32 devices in a mesh: phase: 2 (over x), shard: 16 (over z, y, core).
Axes of the slice: x: 2, y: 2, z: 4, core: 2. Of those that a mesh axis runs over, the one named last changes fastest.
Arguments:
- grid_fields: bfloat16 [2, 128, 128, 512], P(None, 'shard', 'phase'), may hold values from -6 to 6
- encode_weight: bfloat16 [512, 512], replicated, may hold values from -0.25 to 0.25
- encode_send: int32 [16, 16, 3], P('shard'), may hold values from 0 to 7
- encode_count: int32 [16, 16], P('shard'), may hold values from 0 to 3, as said below
- encode_target: int32 [16, 16, 3, 128], P('shard'), may hold values from -1 to 255, as said below
- edge_weight: bfloat16 [2, 512, 1024], P('phase'), may hold values from -0.25 to 0.25
- node_weight: bfloat16 [2, 1024, 512], P('phase'), may hold values from -0.1875 to 0.1875
- node_gain: float32 [2, 512], P('phase'), may hold values from 0.25 to 1.75
- mesh_send: int32 [16, 16, 4], P('shard'), may hold values from 0 to 255
- mesh_neighbour: int32 [4096, 8], P('shard'), may hold values from -1 to 319, as said below
- decode_weight: bfloat16 [512, 512], P(None, 'phase'), may hold values from -0.25 to 0.25
- decode_send: int32 [16, 16, 1], P('shard'), may hold values from 0 to 1
- decode_source: int32 [3, 16384], P(None, 'shard'), may hold values from 0 to 2047
- output_weight: bfloat16 [512, 227], P('phase'), may hold values from -0.25 to 0.25
- skip_weight: bfloat16 [512, 227], replicated, may hold values from -0.25 to 0.25
Outputs:
- forecast: float32 [2, 128, 128, 227], P(None, 'shard', 'phase')
The draws below stay inside these ranges and needn't reach their ends.
Inputs may be any that keep to these rules, and one draw needn't show every extreme that they name: `encode_count`: slots at or past the count hold arbitrary blocks; such slots carry nothing. `encode_target`: -1 marks a row that feeds no node of that owner; entries of slots past the count are arbitrary. `mesh_neighbour`: entries below 256 name the owner's own nodes, larger ones a slot of the node rows received from another owner, -1 no edge.
All inputs are finite; a program needn't handle non-finite values.
Results may differ from the reference program's by a relative error of at most 0.012.
Values may be sent and summed in bfloat16 or wider, within the bound.
A program may use at most 64 MiB of HBM per device.

```python
import jax
import jax.numpy as jnp
from jax import lax

D = 512
DOUT = 227
GB = 8
MN_DEV = 256
M = 2
CAP = 3
CAPM = 4
CAPD = 1
K = 8
BLK = 128
LAYERS = 2
NBLOCKS = 128
GRID = 16384
MESH = 4096
N_SHARD = 16


def draw_encode_send(key, part):
    key = jax.random.fold_in(key, 11)
    blocks = jax.random.randint(key, (N_SHARD, N_SHARD, CAP), 0, GB, dtype=jnp.int32)
    return blocks.at[0, 0, 0].set(GB - 1).at[0, 0, 1].set(0)


def draw_encode_count(key, part):
    key = jax.random.fold_in(key, 12)
    loaded_owner = jax.random.randint(jax.random.fold_in(key, 1), (N_SHARD,), 0, 4, dtype=jnp.int32)
    counts = jax.random.randint(jax.random.fold_in(key, 2), (N_SHARD, N_SHARD), 0, CAP + 1, dtype=jnp.int32)
    counts = jnp.where(loaded_owner[None, :] == 0, CAP, counts)
    return counts.at[0, 0].set(CAP).at[1, 0].set(0)


def draw_encode_target(key, part):
    key = jax.random.fold_in(key, 13)
    chooser = jax.random.randint(jax.random.fold_in(key, 1), (N_SHARD, N_SHARD, CAP, BLK), 0, 4, dtype=jnp.int32)
    node_ids = jax.random.randint(jax.random.fold_in(key, 2), (N_SHARD, N_SHARD, CAP, BLK), 0, MN_DEV, dtype=jnp.int32)
    targets = jnp.where(chooser == 0, -1, node_ids)
    return targets.at[0, 0, 0, 0].set(MN_DEV - 1).at[0, 0, 0, 1].set(-1)


def draw_mesh_send(key, part):
    key = jax.random.fold_in(key, 14)
    node_ids = jax.random.randint(key, (N_SHARD, N_SHARD, CAPM), 0, MN_DEV, dtype=jnp.int32)
    return node_ids.at[0, 0, 0].set(MN_DEV - 1).at[0, 0, 1].set(0)


def draw_mesh_neighbour(key, part):
    key = jax.random.fold_in(key, 15)
    chooser = jax.random.randint(jax.random.fold_in(key, 1), (MESH, K), 0, 8, dtype=jnp.int32)
    side = jax.random.randint(jax.random.fold_in(key, 2), (MESH, K), 0, 2, dtype=jnp.int32)
    local_ids = jax.random.randint(jax.random.fold_in(key, 3), (MESH, K), 0, MN_DEV, dtype=jnp.int32)
    remote_ids = MN_DEV + jax.random.randint(jax.random.fold_in(key, 4), (MESH, K), 0, N_SHARD * CAPM, dtype=jnp.int32)
    entries = jnp.where(chooser == 0, -1, jnp.where(side == 0, local_ids, remote_ids))
    return entries.at[0, 0].set(MN_DEV + N_SHARD * CAPM - 1).at[0, 1].set(-1)


def draw_decode_send(key, part):
    key = jax.random.fold_in(key, 16)
    blocks = jax.random.randint(key, (N_SHARD, N_SHARD, CAPD), 0, MN_DEV // BLK, dtype=jnp.int32)
    return blocks.at[0, 0, 0].set(MN_DEV // BLK - 1).at[1, 0, 0].set(0)


def draw_decode_source(key, part):
    key = jax.random.fold_in(key, 17)
    entries = jax.random.randint(key, (3, GRID), 0, N_SHARD * CAPD * BLK, dtype=jnp.int32)
    return entries.at[0, 0].set(N_SHARD * CAPD * BLK - 1).at[1, 0].set(0)


def block_scale(rng, shape, cuts, smallest, largest):
    gain, own = 1.0, jax.random.fold_in(rng, 6)
    for axis_at, blocks in cuts:
        steps = jnp.exp(jax.random.uniform(jax.random.fold_in(own, axis_at), (blocks,), jnp.float32, smallest / len(cuts), largest / len(cuts)))
        gain = gain * jnp.repeat(steps, shape[axis_at] // blocks).reshape([-1 if axis == axis_at else 1 for axis in range(len(shape))])
    return gain


def bell_draw(rng, shape, width, limit, split=(), kind=jnp.bfloat16):
    values = width * jax.random.normal(rng, shape, jnp.float32)
    if split:
        values = values * block_scale(rng, shape, split, -0.22, 0.18)
    return jnp.clip(values, -limit, limit).astype(kind)


def setup_inputs(seed: int = 0) -> dict:
    splits = jax.random.split(jax.random.key(seed), 16)
    return {
        "grid_fields": bell_draw(splits[0], (M, NBLOCKS, BLK, D), 1.0, 6.0, ((1, 16), (2, 2))),
        "encode_weight": bell_draw(splits[1], (D, D), D ** -0.5, 0.25),
        "encode_send": draw_encode_send(jax.random.fold_in(splits[15], 71), 0),
        "encode_count": draw_encode_count(jax.random.fold_in(splits[15], 71), 0),
        "encode_target": draw_encode_target(jax.random.fold_in(splits[15], 71), 0),
        "edge_weight": bell_draw(splits[5], (LAYERS, D, 2 * D), D ** -0.5, 0.25, ((0, 2),)),
        "node_weight": bell_draw(splits[6], (LAYERS, 2 * D, D), (2 * D) ** -0.5, 0.1875, ((0, 2),)),
        "node_gain": jnp.clip(1.0 + 0.15 * jax.random.normal(splits[7], (LAYERS, D), jnp.float32), 0.25, 1.75),
        "mesh_send": draw_mesh_send(jax.random.fold_in(splits[15], 71), 0),
        "mesh_neighbour": draw_mesh_neighbour(jax.random.fold_in(splits[15], 71), 0),
        "decode_weight": bell_draw(splits[10], (D, D), D ** -0.5, 0.25, ((1, 2),)),
        "decode_send": draw_decode_send(jax.random.fold_in(splits[15], 71), 0),
        "decode_source": draw_decode_source(jax.random.fold_in(splits[15], 71), 0),
        "output_weight": bell_draw(splits[13], (D, DOUT), D ** -0.5, 0.25, ((0, 2),)),
        "skip_weight": bell_draw(splits[14], (D, DOUT), D ** -0.5, 0.25),
    }


def layer_norm(values):
    average = lax.optimization_barrier(jnp.mean(values, axis=-1, keepdims=True))
    centred = values - average
    variance = lax.optimization_barrier(jnp.mean(centred * centred, axis=-1, keepdims=True))
    return centred * lax.rsqrt(variance + 1e-05)

def reference(grid_fields, encode_weight, encode_send, encode_count, encode_target, edge_weight, node_weight, node_gain, mesh_send, mesh_neighbour, decode_weight, decode_send, decode_source, output_weight, skip_weight):
    grid_rows = grid_fields.reshape(M * NBLOCKS * BLK, D)
    messages = jax.nn.silu(jnp.dot(grid_rows, encode_weight, preferred_element_type=jnp.float32)).astype(jnp.bfloat16)
    messages = messages.reshape(M, N_SHARD, GB, BLK, D)
    slot_ids = jnp.arange(CAP, dtype=jnp.int32)
    sender_ids = jnp.arange(N_SHARD, dtype=jnp.int32)

    def encode_owner(owner):
        blocks_sent = encode_send[:, owner, :]
        live = slot_ids[None, :] < encode_count[:, owner][:, None]
        picked = messages[:, sender_ids[:, None], blocks_sent]
        targets = encode_target[owner]
        node_ids = jnp.where(live[:, :, None] & (targets >= 0), targets, MN_DEV).reshape(-1).astype(jnp.int32)

        def one_batch(batch_rows):
            return jax.ops.segment_sum(batch_rows.reshape(-1, D).astype(jnp.float32), node_ids, num_segments=MN_DEV + 1)[:MN_DEV]
        return jax.vmap(one_batch)(picked)
    encoded = lax.map(encode_owner, jnp.arange(N_SHARD, dtype=jnp.int32))
    encoded = jnp.transpose(encoded, (1, 0, 2, 3)).reshape(M, MESH, D)
    states = layer_norm(encoded).astype(jnp.bfloat16)
    owners = jnp.arange(MESH, dtype=jnp.int32) // MN_DEV
    remote_pos = jnp.clip(mesh_neighbour - MN_DEV, 0, N_SHARD * CAPM - 1)
    remote_owner = remote_pos // CAPM
    remote_slot = remote_pos % CAPM
    remote_node = remote_owner * MN_DEV + mesh_send[remote_owner, owners[:, None], remote_slot]
    local_node = owners[:, None] * MN_DEV + jnp.clip(mesh_neighbour, 0, MN_DEV - 1)
    sources = jnp.where(mesh_neighbour < MN_DEV, local_node, remote_node).astype(jnp.int32)
    edge_live = mesh_neighbour >= 0
    for layer in range(LAYERS):
        both_parts = jnp.dot(states.reshape(M * MESH, D), edge_weight[layer], preferred_element_type=jnp.float32).reshape(M, MESH, 2 * D)
        source_part = both_parts[..., :D].astype(jnp.bfloat16)
        dest_part = both_parts[..., D:]
        running = jnp.zeros((M, MESH, D), jnp.float32)
        for slot_index in range(K):
            gathered = source_part[:, sources[:, slot_index]].astype(jnp.float32)
            running = running + jnp.where(edge_live[:, slot_index][None, :, None], jax.nn.silu(gathered + dest_part), 0.0)
        summary = running.astype(jnp.bfloat16)
        joined = jnp.concatenate([states, summary], axis=-1).reshape(M * MESH, 2 * D)
        mixed = jnp.dot(joined, node_weight[layer], preferred_element_type=jnp.float32).reshape(M, MESH, D)
        states = (states.astype(jnp.float32) + node_gain[layer] * layer_norm(jax.nn.silu(mixed))).astype(jnp.bfloat16)
    mapped = jnp.dot(states.reshape(M * MESH, D), decode_weight, preferred_element_type=jnp.float32).astype(jnp.bfloat16).reshape(M, MESH, D)
    cell_ids = jnp.arange(GRID, dtype=jnp.int32)
    grid_owner = cell_ids // (GB * BLK)
    picked_owner = decode_source // (CAPD * BLK)
    picked_slot = decode_source // BLK % CAPD
    picked_row = decode_source % BLK
    node_index = (picked_owner * MN_DEV + decode_send[picked_owner, grid_owner[None, :], picked_slot] * BLK + picked_row).astype(jnp.int32)
    summed = mapped[:, node_index[0]].astype(jnp.float32)
    summed = summed + mapped[:, node_index[1]].astype(jnp.float32)
    summed = summed + mapped[:, node_index[2]].astype(jnp.float32)
    hidden = jax.nn.silu(summed).astype(jnp.bfloat16)
    result = jnp.dot(hidden.reshape(M * GRID, D), output_weight, preferred_element_type=jnp.float32)
    result = result + jnp.dot(grid_rows, skip_weight, preferred_element_type=jnp.float32)
    return result.reshape(M, NBLOCKS, BLK, DOUT)
```

```python
import math

import jax
import jax.numpy as jnp
from jax import lax
from jax.sharding import PartitionSpec as P


def from_behind(value, axis, by):
    length = lax.axis_size(axis)
    pairs = [(i, i + by) for i in range(length) if 0 <= i + by < length]
    return lax.ppermute(value, axis, pairs)


def broadcast(block, axis, source):
    block = jnp.where(lax.axis_index(axis) == source, block, jnp.zeros_like(block))
    return lax.psum(block, axis)


def layer_norm(values):
    average = jnp.mean(values, axis=-1, keepdims=True)
    centred = values - average
    variance = jnp.mean(centred * centred, axis=-1, keepdims=True)
    return centred * lax.rsqrt(variance + 1e-05)


def add_by_target(values, targets, node_count):
    row_count, columns = values.shape
    block_rows = math.gcd(row_count, 2048)
    value_blocks = values.reshape(row_count // block_rows, block_rows, columns)
    target_blocks = targets.reshape(row_count // block_rows, block_rows)
    node_ids = jnp.arange(node_count, dtype=jnp.int32)

    def accumulate(running, pieces):
        onehot = (pieces[1][None, :] == node_ids[:, None]).astype(jnp.bfloat16)
        return (running + jnp.dot(onehot, pieces[0], preferred_element_type=jnp.float32), None)

    running, unused = lax.scan(
        accumulate, jnp.zeros((node_count, columns), jnp.float32), (value_blocks, target_blocks)
    )
    return running


def encode_sums(messages, send_blocks, slot_live, targets, node_count):
    picked = messages[send_blocks]
    picked = jnp.where(slot_live[:, :, None, None, None], picked, jnp.zeros_like(picked))
    arrived = lax.all_to_all(picked, "shard", split_axis=0, concat_axis=0, tiled=True)
    peer_count, capacity, part_rows, batches, columns = arrived.shape
    node_ids = jnp.where(targets >= 0, targets, node_count).reshape(-1)
    summed = add_by_target(
        arrived.reshape(peer_count * capacity * part_rows, batches * columns), node_ids, node_count
    )
    return jnp.transpose(summed.reshape(node_count, batches, columns), (1, 0, 2))


def on_device_sections(
    grid_fields,
    encode_weight,
    encode_send,
    encode_count,
    encode_target,
    edge_weight,
    node_weight,
    node_gain,
    mesh_send,
    mesh_neighbour,
    decode_weight,
    decode_send,
    decode_source,
    output_weight,
    skip_weight,
):
    phases = lax.axis_size("phase")
    phase_index = lax.axis_index("phase")
    batches, blocks, part_rows, features = grid_fields.shape
    node_count = mesh_neighbour.shape[0]
    block_size = encode_target.shape[3]
    send_blocks = encode_send[0]
    capacity = send_blocks.shape[1]
    slot_live = jnp.arange(capacity, dtype=jnp.int32)[None, :] < encode_count[0][:, None]
    messages = jax.nn.silu(
        jnp.einsum("mgrd,dc->grmc", grid_fields, encode_weight, preferred_element_type=jnp.float32)
    ).astype(jnp.bfloat16)
    own_targets = lax.dynamic_slice_in_dim(encode_target[0], phase_index * part_rows, part_rows, 2)
    partial_sums = encode_sums(messages, send_blocks, slot_live, own_targets, node_count)
    encoded = lax.psum(partial_sums, "phase")
    initial = layer_norm(encoded).astype(jnp.bfloat16)
    my_edge = edge_weight[0]
    my_node = node_weight[0]
    my_gain = node_gain[0]
    send_nodes = mesh_send[0]
    edge_live = mesh_neighbour >= 0
    safe_index = jnp.where(edge_live, mesh_neighbour, 0)
    slot_count = mesh_neighbour.shape[1]

    def process(mesh_state):
        both_parts = jnp.dot(mesh_state, my_edge, preferred_element_type=jnp.float32)
        source_part = both_parts[:, :features].astype(jnp.bfloat16)
        dest_part = both_parts[:, features:]
        incoming = lax.all_to_all(
            source_part[send_nodes], "shard", split_axis=0, concat_axis=0, tiled=True
        )
        lookup_table = jnp.concatenate([source_part, incoming.reshape(-1, features)], axis=0)
        running = jnp.zeros((node_count, features), jnp.float32)
        for slot_index in range(slot_count):
            gathered = lookup_table[safe_index[:, slot_index]].astype(jnp.float32)
            running = running + jnp.where(
                edge_live[:, slot_index][:, None], jax.nn.silu(gathered + dest_part), 0.0
            )
        summary = running.astype(jnp.bfloat16)
        mixed = jnp.dot(mesh_state, my_node[:features], preferred_element_type=jnp.float32)
        mixed = mixed + jnp.dot(summary, my_node[features:], preferred_element_type=jnp.float32)
        return (mesh_state.astype(jnp.float32) + my_gain * layer_norm(jax.nn.silu(mixed))).astype(
            jnp.bfloat16
        )

    tick_count = batches + phases - 1

    def advance(carried, tick_index):
        current, finished = carried
        entering = lax.dynamic_index_in_dim(
            initial, jnp.minimum(tick_index, batches - 1), 0, keepdims=False
        )
        inputs = jnp.where(phase_index == 0, entering, current)
        result = process(inputs)
        leaving = tick_index - (phases - 1)
        updated = lax.dynamic_update_index_in_dim(finished, result, jnp.maximum(leaving, 0), 0)
        finished = jnp.where((phase_index == phases - 1) & (leaving >= 0), updated, finished)
        current = from_behind(result, "phase", 1)
        return ((current, finished), None)

    carried, unused = lax.scan(
        advance,
        (jnp.zeros_like(initial[0]), jnp.zeros_like(initial)),
        jnp.arange(tick_count, dtype=jnp.int32),
    )
    finished = carried[1]
    final_states = broadcast(finished, "phase", phases - 1)
    mapped = jnp.einsum(
        "mnd,dc->nmc", final_states, decode_weight, preferred_element_type=jnp.float32
    ).astype(jnp.bfloat16)
    columns = mapped.shape[2]
    node_blocks = mapped.reshape(node_count // block_size, block_size, batches, columns)
    outgoing = node_blocks[decode_send[0]]
    arrived = lax.all_to_all(outgoing, "shard", split_axis=0, concat_axis=0, tiled=True)
    arrived = arrived.reshape(-1, batches, columns)
    summed = arrived[decode_source[0]].astype(jnp.float32)
    summed = summed + arrived[decode_source[1]].astype(jnp.float32)
    summed = summed + arrived[decode_source[2]].astype(jnp.float32)
    hidden = jax.nn.silu(summed).astype(jnp.bfloat16)
    skipped = jnp.einsum(
        "mgrd,do->mgro", grid_fields, skip_weight, preferred_element_type=jnp.float32
    )
    output_terms = jnp.einsum(
        "rmc,co->mro", hidden, output_weight, preferred_element_type=jnp.float32
    )
    output_terms = output_terms.reshape(batches, blocks, block_size, output_terms.shape[2])
    shared = lax.psum_scatter(output_terms, "phase", scatter_dimension=2, tiled=True)
    return shared + skipped


def swap(value):
    return lax.ppermute(value, "phase", [(0, 1), (1, 0)])


def sum_to_owners(partial_sums):
    return lax.psum_scatter(partial_sums, "shard", scatter_dimension=0, tiled=True)[0]


def gather_nodes(mapped):
    return lax.all_gather(mapped, "shard", axis=0, tiled=False)


def one_hot(indices, count, live):
    hot = (indices[..., None] == jnp.arange(count, dtype=jnp.int32)) & live[..., None]
    return hot.astype(jnp.bfloat16)


def on_device_batches(
    grid_fields,
    encode_weight,
    encode_send,
    encode_count,
    encode_target,
    edge_weight,
    node_weight,
    node_gain,
    mesh_send,
    mesh_neighbour,
    decode_weight,
    decode_send,
    decode_source,
    output_weight,
    skip_weight,
):
    phase_index = lax.axis_index("phase")
    owners = lax.axis_size("shard")
    batches, blocks, part_rows, features = grid_fields.shape
    node_count, slot_count = mesh_neighbour.shape
    block_size = encode_target.shape[3]
    send_blocks = encode_send[0]
    capacity = send_blocks.shape[1]

    messages = jax.nn.silu(
        jnp.einsum("mgrd,dc->mgrc", grid_fields, encode_weight, preferred_element_type=jnp.float32)
    ).astype(jnp.bfloat16)
    own = lax.dynamic_index_in_dim(messages, phase_index, 0, keepdims=False)
    away = lax.dynamic_index_in_dim(messages, 1 - phase_index, 0, keepdims=False)
    came = swap(away)
    rows = jnp.concatenate([own, came], axis=1)

    tables = jnp.concatenate(
        [encode_target[0].reshape(owners, -1), decode_send[0].reshape(owners, -1)], axis=1
    )
    tables = lax.all_to_all(tables, "shard", split_axis=0, concat_axis=0, tiled=True)
    targets = tables[:, : capacity * block_size].reshape(owners, capacity, 2, part_rows)
    decode_block = tables[:, capacity * block_size :]
    targets = jnp.where(phase_index == 0, targets, targets[:, :, ::-1])
    targets = targets.reshape(owners, capacity * block_size)
    slot_live = jnp.arange(capacity, dtype=jnp.int32)[None, :] < encode_count[0][:, None]
    live = jnp.repeat(slot_live, block_size, axis=1)
    targets = jnp.where(live, targets, -1)
    hot = targets[:, None, :] == jnp.arange(node_count, dtype=jnp.int32)[None, :, None]
    picked = rows[send_blocks].reshape(owners, capacity * block_size, features)
    partial_sums = jnp.einsum(
        "onr,orc->onc", hot.astype(jnp.bfloat16), picked, preferred_element_type=jnp.float32
    ).astype(jnp.bfloat16)
    encoded = sum_to_owners(partial_sums).astype(jnp.float32)
    states = layer_norm(encoded).astype(jnp.bfloat16)

    other_edge, other_node, other_gain = swap(edge_weight[0]), swap(node_weight[0]), swap(node_gain[0])
    decode_all = jnp.concatenate([decode_weight, swap(decode_weight)], axis=1)
    output_all = jnp.concatenate([output_weight, swap(output_weight)], axis=0)

    edge_live = mesh_neighbour.T >= 0
    remote = owners * mesh_send.shape[2]
    source_hot = one_hot(mesh_neighbour.T, node_count + remote, edge_live)
    send_nodes = mesh_send[0].reshape(-1)
    send_hot = one_hot(send_nodes, node_count, send_nodes >= 0)
    for layer in range(2):
        mine = phase_index == layer
        edge = jnp.where(mine, edge_weight[0], other_edge)
        node = jnp.where(mine, node_weight[0], other_node)
        gain = jnp.where(mine, node_gain[0], other_gain)
        both_parts = jnp.dot(states, edge, preferred_element_type=jnp.float32)
        source_part = both_parts[:, :features].astype(jnp.bfloat16)
        dest_part = both_parts[:, features:]
        outgoing = jnp.dot(send_hot, source_part, preferred_element_type=jnp.float32)
        outgoing = outgoing.astype(jnp.bfloat16).reshape(owners, -1, features)
        incoming = lax.all_to_all(outgoing, "shard", split_axis=0, concat_axis=0, tiled=True)
        table = jnp.concatenate([source_part, incoming.reshape(-1, features)], axis=0)
        running = jnp.zeros((node_count, features), jnp.float32)
        for slot_index in range(slot_count):
            gathered = jnp.dot(source_hot[slot_index], table, preferred_element_type=jnp.float32)
            running = running + jnp.where(
                edge_live[slot_index][:, None], jax.nn.silu(gathered + dest_part), 0.0
            )
        summary = running.astype(jnp.bfloat16)
        mixed = jnp.dot(states, node[:features], preferred_element_type=jnp.float32)
        mixed = mixed + jnp.dot(summary, node[features:], preferred_element_type=jnp.float32)
        states = (states.astype(jnp.float32) + gain * layer_norm(jax.nn.silu(mixed))).astype(
            jnp.bfloat16
        )
    mapped = jnp.dot(states, decode_all, preferred_element_type=jnp.float32).astype(jnp.bfloat16)

    gathered = gather_nodes(mapped).reshape(owners, node_count // block_size, block_size, features)
    chosen = gathered[jnp.arange(owners), decode_block[:, 0]].reshape(owners * block_size, features)
    cells = decode_source.reshape(3, blocks, 2, part_rows)

    def outputs(half):
        indices = lax.dynamic_index_in_dim(cells, half, 2, keepdims=False).reshape(3, -1)
        ids = jnp.arange(owners * block_size, dtype=jnp.int32)[None, :]
        counts = sum((indices[e][:, None] == ids).astype(jnp.float32) for e in range(3))
        summed = jnp.dot(counts.astype(jnp.bfloat16), chosen, preferred_element_type=jnp.float32)
        hidden = jax.nn.silu(summed).astype(jnp.bfloat16)
        return jnp.dot(hidden, output_all, preferred_element_type=jnp.float32)

    leaving = outputs(1 - phase_index).astype(jnp.bfloat16)
    arriving = swap(leaving).astype(jnp.float32)
    kept = outputs(phase_index)
    skipped = jnp.einsum(
        "mgrd,do->mgro", grid_fields, skip_weight, preferred_element_type=jnp.float32
    )
    here = (jnp.arange(2) == phase_index)[:, None, None, None]
    shape = (1, blocks, part_rows, kept.shape[1])
    return jnp.where(here, kept.reshape(shape), arriving.reshape(shape)) + skipped


def on_device(grid_fields, *others):
    phases, batches = lax.axis_size("phase"), grid_fields.shape[0]
    if phases == batches == 2 and others[10].shape[2] == 1:
        return on_device_batches(grid_fields, *others)
    return on_device_sections(grid_fields, *others)


def solution(mesh):
    return jax.shard_map(
        on_device,
        mesh=mesh,
        in_specs=(
            P(None, "shard", "phase", None),
            P(),
            P("shard", None, None),
            P("shard", None),
            P("shard", None, None, None),
            P("phase", None, None),
            P("phase", None, None),
            P("phase", None),
            P("shard", None, None),
            P("shard", None),
            P(None, "phase"),
            P("shard", None, None),
            P(None, "shard"),
            P("phase", None),
            P(),
        ),
        out_specs=P(None, "shard", "phase", None),
        check_vma=False,
    )
```

```python
import math

import jax
import jax.numpy as jnp
from jax import lax
from jax.experimental import pallas as pl
from jax.experimental.pallas import tpu as pltpu
from jax.sharding import PartitionSpec as P


def from_behind(value, axis, by):
    length = lax.axis_size(axis)
    pairs = [(i, i + by) for i in range(length) if 0 <= i + by < length]
    return lax.ppermute(value, axis, pairs)


def broadcast(block, axis, source):
    block = jnp.where(lax.axis_index(axis) == source, block, jnp.zeros_like(block))
    return lax.psum(block, axis)


def layer_norm(values):
    average = jnp.mean(values, axis=-1, keepdims=True)
    centred = values - average
    variance = jnp.mean(centred * centred, axis=-1, keepdims=True)
    return centred * lax.rsqrt(variance + 1e-05)


def add_by_target(values, targets, node_count):
    row_count, columns = values.shape
    block_rows = math.gcd(row_count, 2048)
    value_blocks = values.reshape(row_count // block_rows, block_rows, columns)
    target_blocks = targets.reshape(row_count // block_rows, block_rows)
    node_ids = jnp.arange(node_count, dtype=jnp.int32)

    def accumulate(running, pieces):
        onehot = (pieces[1][None, :] == node_ids[:, None]).astype(jnp.bfloat16)
        return (running + jnp.dot(onehot, pieces[0], preferred_element_type=jnp.float32), None)

    running, unused = lax.scan(
        accumulate, jnp.zeros((node_count, columns), jnp.float32), (value_blocks, target_blocks)
    )
    return running


def encode_sums(messages, send_blocks, slot_live, targets, node_count):
    picked = messages[send_blocks]
    picked = jnp.where(slot_live[:, :, None, None, None], picked, jnp.zeros_like(picked))
    arrived = lax.all_to_all(picked, "shard", split_axis=0, concat_axis=0, tiled=True)
    peer_count, capacity, part_rows, batches, columns = arrived.shape
    node_ids = jnp.where(targets >= 0, targets, node_count).reshape(-1)
    summed = add_by_target(
        arrived.reshape(peer_count * capacity * part_rows, batches * columns), node_ids, node_count
    )
    return jnp.transpose(summed.reshape(node_count, batches, columns), (1, 0, 2))


def on_device_sections(
    grid_fields,
    encode_weight,
    encode_send,
    encode_count,
    encode_target,
    edge_weight,
    node_weight,
    node_gain,
    mesh_send,
    mesh_neighbour,
    decode_weight,
    decode_send,
    decode_source,
    output_weight,
    skip_weight,
):
    phases = lax.axis_size("phase")
    phase_index = lax.axis_index("phase")
    batches, blocks, part_rows, features = grid_fields.shape
    node_count = mesh_neighbour.shape[0]
    block_size = encode_target.shape[3]
    send_blocks = encode_send[0]
    capacity = send_blocks.shape[1]
    slot_live = jnp.arange(capacity, dtype=jnp.int32)[None, :] < encode_count[0][:, None]
    messages = jax.nn.silu(
        jnp.einsum("mgrd,dc->grmc", grid_fields, encode_weight, preferred_element_type=jnp.float32)
    ).astype(jnp.bfloat16)
    own_targets = lax.dynamic_slice_in_dim(encode_target[0], phase_index * part_rows, part_rows, 2)
    partial_sums = encode_sums(messages, send_blocks, slot_live, own_targets, node_count)
    encoded = lax.psum(partial_sums, "phase")
    initial = layer_norm(encoded).astype(jnp.bfloat16)
    my_edge = edge_weight[0]
    my_node = node_weight[0]
    my_gain = node_gain[0]
    send_nodes = mesh_send[0]
    edge_live = mesh_neighbour >= 0
    safe_index = jnp.where(edge_live, mesh_neighbour, 0)
    slot_count = mesh_neighbour.shape[1]

    def process(mesh_state):
        both_parts = jnp.dot(mesh_state, my_edge, preferred_element_type=jnp.float32)
        source_part = both_parts[:, :features].astype(jnp.bfloat16)
        dest_part = both_parts[:, features:]
        incoming = lax.all_to_all(
            source_part[send_nodes], "shard", split_axis=0, concat_axis=0, tiled=True
        )
        lookup_table = jnp.concatenate([source_part, incoming.reshape(-1, features)], axis=0)
        running = jnp.zeros((node_count, features), jnp.float32)
        for slot_index in range(slot_count):
            gathered = lookup_table[safe_index[:, slot_index]].astype(jnp.float32)
            running = running + jnp.where(
                edge_live[:, slot_index][:, None], jax.nn.silu(gathered + dest_part), 0.0
            )
        summary = running.astype(jnp.bfloat16)
        mixed = jnp.dot(mesh_state, my_node[:features], preferred_element_type=jnp.float32)
        mixed = mixed + jnp.dot(summary, my_node[features:], preferred_element_type=jnp.float32)
        return (mesh_state.astype(jnp.float32) + my_gain * layer_norm(jax.nn.silu(mixed))).astype(
            jnp.bfloat16
        )

    tick_count = batches + phases - 1

    def advance(carried, tick_index):
        current, finished = carried
        entering = lax.dynamic_index_in_dim(
            initial, jnp.minimum(tick_index, batches - 1), 0, keepdims=False
        )
        inputs = jnp.where(phase_index == 0, entering, current)
        result = process(inputs)
        leaving = tick_index - (phases - 1)
        updated = lax.dynamic_update_index_in_dim(finished, result, jnp.maximum(leaving, 0), 0)
        finished = jnp.where((phase_index == phases - 1) & (leaving >= 0), updated, finished)
        current = from_behind(result, "phase", 1)
        return ((current, finished), None)

    carried, unused = lax.scan(
        advance,
        (jnp.zeros_like(initial[0]), jnp.zeros_like(initial)),
        jnp.arange(tick_count, dtype=jnp.int32),
    )
    finished = carried[1]
    final_states = broadcast(finished, "phase", phases - 1)
    mapped = jnp.einsum(
        "mnd,dc->nmc", final_states, decode_weight, preferred_element_type=jnp.float32
    ).astype(jnp.bfloat16)
    columns = mapped.shape[2]
    node_blocks = mapped.reshape(node_count // block_size, block_size, batches, columns)
    outgoing = node_blocks[decode_send[0]]
    arrived = lax.all_to_all(outgoing, "shard", split_axis=0, concat_axis=0, tiled=True)
    arrived = arrived.reshape(-1, batches, columns)
    summed = arrived[decode_source[0]].astype(jnp.float32)
    summed = summed + arrived[decode_source[1]].astype(jnp.float32)
    summed = summed + arrived[decode_source[2]].astype(jnp.float32)
    hidden = jax.nn.silu(summed).astype(jnp.bfloat16)
    skipped = jnp.einsum(
        "mgrd,do->mgro", grid_fields, skip_weight, preferred_element_type=jnp.float32
    )
    output_terms = jnp.einsum(
        "rmc,co->mro", hidden, output_weight, preferred_element_type=jnp.float32
    )
    output_terms = output_terms.reshape(batches, blocks, block_size, output_terms.shape[2])
    shared = lax.psum_scatter(output_terms, "phase", scatter_dimension=2, tiled=True)
    return shared + skipped


def swap(value):
    return lax.ppermute(value, "phase", [(0, 1), (1, 0)])


MESH_ID = pl.DeviceIdType.MESH
DEPTH, ROWS, CORES = 4, 2, 2


def greet(peers):
    barrier = pltpu.get_barrier_semaphore()
    for peer in peers:
        pl.semaphore_signal(barrier, inc=1, device_id=peer, device_id_type=MESH_ID)
    pl.semaphore_wait(barrier, len(peers))


def send(source, target, sems, at, peer):
    copy = pltpu.make_async_remote_copy(
        src_ref=source,
        dst_ref=target,
        send_sem=sems.at[0, at],
        recv_sem=sems.at[1, at],
        device_id=peer,
        device_id_type=MESH_ID,
    )
    copy.start()
    return copy


def places():
    phase, me = lax.axis_index("phase"), lax.axis_index("shard")
    z, y, c = me // 4, (me // 2) % 2, me % 2

    def at(z, y, c):
        return (phase, z * 4 + y * 2 + c)

    across = at(z, y, 1 - c)
    beside = at(z, 1 - y, c)
    line = [at((z + k) % DEPTH, y, c) for k in range(1, DEPTH)]
    return phase, me, z, y, c, across, beside, line


def owner_kernel(
    part, edge, node, states, edges, nodes,
    core_in, y_out, y_in, z_out, z_in, total, core_sems, y_sems, z_sems, weight_sems,
):
    phase, me, z, y, c, across, beside, line = places()
    partner = (1 - phase, me)
    greet([across, beside, partner] + line)
    step = 32
    tiles = part.shape[3] // step
    order = (2, 1, 3, 0)
    spots = [(z + k) % DEPTH for k in range(DEPTH)]
    core_copies = {}
    for k in order:
        core_copies[k] = send(
            part.at[spots[k], :, 1 - c], core_in.at[spots[k]], core_sems, k, across
        )
    weight_copies = [
        send(edge, edges.at[c], weight_sems, 0, partner),
        send(node, nodes.at[c], weight_sems, 1, partner),
    ]

    def over_tiles(body):
        def run(t, carry):
            body(pl.ds(pl.multiple_of(t * step, step), step))
            return carry

        lax.fori_loop(0, tiles, run, 0)

    def pair(spot, row, at):
        return part[spot, row, c, at, :].astype(jnp.float32) + core_in[spot, row, at, :].astype(
            jnp.float32
        )

    y_copies = {}
    for k in order:
        core_copies[k].wait()
        spot = spots[k]

        def to_beside(at):
            y_out[k, at, :] = pair(spot, 1 - y, at).astype(jnp.bfloat16)

        over_tiles(to_beside)
        y_copies[k] = send(y_out.at[k], y_in.at[k], y_sems, k, beside)
    z_copies = []
    for k in order:
        y_copies[k].wait()
        spot = spots[k]

        def add_up(at):
            value = pair(spot, y, at) + y_in[k, at, :].astype(jnp.float32)
            if k == 0:
                total[at, :] = value
            else:
                z_out[k - 1, at, :] = value.astype(jnp.bfloat16)

        over_tiles(add_up)
        if k:
            z_copies.append(send(z_out.at[k - 1], z_in.at[k - 1], z_sems, k - 1, line[k - 1]))
    for copy in weight_copies:
        copy.wait()
    weight_copies = [
        send(edges.at[c], edges.at[c], weight_sems, 2, across),
        send(nodes.at[c], nodes.at[c], weight_sems, 3, across),
    ]
    for copy in z_copies:
        copy.wait()

    def finish(at):
        value = total[at, :]
        for k in range(DEPTH - 1):
            value = value + z_in[k, at, :].astype(jnp.float32)
        states[at, :] = layer_norm(value).astype(jnp.bfloat16)

    over_tiles(finish)
    for copy in weight_copies:
        copy.wait()


def states_and_weights(partial_sums, edge, node):
    owners, nodes, features = partial_sums.shape
    part = partial_sums.reshape(DEPTH, ROWS, CORES, nodes, features)
    core = lax.axis_index("shard") % 2
    edge_half = lax.dynamic_index_in_dim(
        edge.reshape(2, edge.shape[0] // 2, edge.shape[1]), core, 0, keepdims=False
    )
    node_half = lax.dynamic_index_in_dim(
        node.reshape(2, node.shape[0] // 2, node.shape[1]), core, 0, keepdims=False
    )
    kind = jnp.bfloat16
    states, edges, node_weights = pl.pallas_call(
        owner_kernel,
        out_shape=(
            jax.ShapeDtypeStruct((nodes, features), kind),
            jax.ShapeDtypeStruct((2,) + edge_half.shape, kind),
            jax.ShapeDtypeStruct((2,) + node_half.shape, kind),
        ),
        in_specs=[pl.BlockSpec(memory_space=pltpu.VMEM)] * 3,
        out_specs=[pl.BlockSpec(memory_space=pltpu.VMEM)] * 3,
        scratch_shapes=[
            pltpu.VMEM((DEPTH, ROWS, nodes, features), kind),
            pltpu.VMEM((DEPTH, nodes, features), kind),
            pltpu.VMEM((DEPTH, nodes, features), kind),
            pltpu.VMEM((DEPTH - 1, nodes, features), kind),
            pltpu.VMEM((DEPTH - 1, nodes, features), kind),
            pltpu.VMEM((nodes, features), jnp.float32),
            pltpu.SemaphoreType.DMA((2, DEPTH)),
            pltpu.SemaphoreType.DMA((2, DEPTH)),
            pltpu.SemaphoreType.DMA((2, DEPTH - 1)),
            pltpu.SemaphoreType.DMA((2, 4)),
        ],
        compiler_params=pltpu.CompilerParams(
            collective_id=0, has_side_effects=True, vmem_limit_bytes=40 * 2**20
        ),
        name="sum_to_owners",
    )(part, edge_half, node_half)
    return states, edges.reshape(edge.shape), node_weights.reshape(node.shape)


def gather_kernel(mine, everyone, own_sem, z_sems, y_sems, core_sems):
    phase, me, z, y, c, across, beside, line = places()
    greet([across, beside] + line)
    here = everyone.at[z, y, c]
    z_copies = {}
    for k in (1, 3, 2):
        z_copies[k] = send(mine, here, z_sems, k - 1, line[k - 1])
    y_copies = {0: send(mine, here, y_sems, 0, beside)}
    core_copies = [send(mine, here, core_sems, 0, across)]
    keep = pltpu.make_async_copy(mine, here, own_sem.at[0])
    keep.start()
    for k in (1, 3, 2):
        z_copies[k].wait()
        block = everyone.at[(z + DEPTH - k) % DEPTH, y, c]
        y_copies[k] = send(block, block, y_sems, k, beside)
        core_copies.append(send(block, block, core_sems, k, across))
    for k in (0, 1, 3, 2):
        y_copies[k].wait()
        block = everyone.at[(z + DEPTH - k) % DEPTH, 1 - y, c]
        core_copies.append(send(block, block, core_sems, DEPTH + k, across))
    keep.wait()
    for copy in core_copies:
        copy.wait()


def gather_nodes(mapped):
    return pl.pallas_call(
        gather_kernel,
        out_shape=jax.ShapeDtypeStruct((DEPTH, ROWS, CORES) + mapped.shape, mapped.dtype),
        in_specs=[pl.BlockSpec(memory_space=pltpu.VMEM)],
        out_specs=pl.BlockSpec(memory_space=pltpu.VMEM),
        scratch_shapes=[
            pltpu.SemaphoreType.DMA((1,)),
            pltpu.SemaphoreType.DMA((2, DEPTH - 1)),
            pltpu.SemaphoreType.DMA((2, DEPTH)),
            pltpu.SemaphoreType.DMA((2, 2 * DEPTH)),
        ],
        compiler_params=pltpu.CompilerParams(
            collective_id=1, has_side_effects=True, vmem_limit_bytes=24 * 2**20
        ),
        name="gather_nodes",
    )(mapped)


def one_hot(indices, count, live):
    hot = (indices[..., None] == jnp.arange(count, dtype=jnp.int32)) & live[..., None]
    return hot.astype(jnp.bfloat16)


def on_device_batches(
    grid_fields,
    encode_weight,
    encode_send,
    encode_count,
    encode_target,
    edge_weight,
    node_weight,
    node_gain,
    mesh_send,
    mesh_neighbour,
    decode_weight,
    decode_send,
    decode_source,
    output_weight,
    skip_weight,
):
    phase_index = lax.axis_index("phase")
    owners = lax.axis_size("shard")
    batches, blocks, part_rows, features = grid_fields.shape
    node_count, slot_count = mesh_neighbour.shape
    block_size = encode_target.shape[3]
    send_blocks = encode_send[0]
    capacity = send_blocks.shape[1]

    messages = jax.nn.silu(
        jnp.einsum("mgrd,dc->mgrc", grid_fields, encode_weight, preferred_element_type=jnp.float32)
    ).astype(jnp.bfloat16)
    own = lax.dynamic_index_in_dim(messages, phase_index, 0, keepdims=False)
    away = lax.dynamic_index_in_dim(messages, 1 - phase_index, 0, keepdims=False)
    came = swap(away)
    rows = jnp.concatenate([own, came], axis=1)

    tables = jnp.concatenate(
        [encode_target[0].reshape(owners, -1), decode_send[0].reshape(owners, -1)], axis=1
    )
    tables = lax.all_to_all(tables, "shard", split_axis=0, concat_axis=0, tiled=True)
    targets = tables[:, : capacity * block_size].reshape(owners, capacity, 2, part_rows)
    decode_block = tables[:, capacity * block_size :]
    targets = jnp.where(phase_index == 0, targets, targets[:, :, ::-1])
    targets = targets.reshape(owners, capacity * block_size)
    slot_live = jnp.arange(capacity, dtype=jnp.int32)[None, :] < encode_count[0][:, None]
    live = jnp.repeat(slot_live, block_size, axis=1)
    targets = jnp.where(live, targets, -1)
    hot = targets[:, None, :] == jnp.arange(node_count, dtype=jnp.int32)[None, :, None]
    picked = rows[send_blocks].reshape(owners, capacity * block_size, features)
    partial_sums = jnp.einsum(
        "onr,orc->onc", hot.astype(jnp.bfloat16), picked, preferred_element_type=jnp.float32
    ).astype(jnp.bfloat16)
    states, other_edge, other_node = states_and_weights(
        partial_sums, edge_weight[0], node_weight[0]
    )
    other_gain = swap(node_gain[0])
    decode_all = jnp.concatenate([decode_weight, swap(decode_weight)], axis=1)
    output_all = jnp.concatenate([output_weight, swap(output_weight)], axis=0)

    edge_live = mesh_neighbour.T >= 0
    remote = owners * mesh_send.shape[2]
    source_hot = one_hot(mesh_neighbour.T, node_count + remote, edge_live)
    send_nodes = mesh_send[0].reshape(-1)
    send_hot = one_hot(send_nodes, node_count, send_nodes >= 0)
    for layer in range(2):
        mine = phase_index == layer
        edge = jnp.where(mine, edge_weight[0], other_edge)
        node = jnp.where(mine, node_weight[0], other_node)
        gain = jnp.where(mine, node_gain[0], other_gain)
        both_parts = jnp.dot(states, edge, preferred_element_type=jnp.float32)
        source_part = both_parts[:, :features].astype(jnp.bfloat16)
        dest_part = both_parts[:, features:]
        outgoing = jnp.dot(send_hot, source_part, preferred_element_type=jnp.float32)
        outgoing = outgoing.astype(jnp.bfloat16).reshape(owners, -1, features)
        incoming = lax.all_to_all(outgoing, "shard", split_axis=0, concat_axis=0, tiled=True)
        table = jnp.concatenate([source_part, incoming.reshape(-1, features)], axis=0)
        running = jnp.zeros((node_count, features), jnp.float32)
        for slot_index in range(slot_count):
            gathered = jnp.dot(source_hot[slot_index], table, preferred_element_type=jnp.float32)
            running = running + jnp.where(
                edge_live[slot_index][:, None], jax.nn.silu(gathered + dest_part), 0.0
            )
        summary = running.astype(jnp.bfloat16)
        mixed = jnp.dot(states, node[:features], preferred_element_type=jnp.float32)
        mixed = mixed + jnp.dot(summary, node[features:], preferred_element_type=jnp.float32)
        states = (states.astype(jnp.float32) + gain * layer_norm(jax.nn.silu(mixed))).astype(
            jnp.bfloat16
        )
    mapped = jnp.dot(states, decode_all, preferred_element_type=jnp.float32).astype(jnp.bfloat16)

    gathered = gather_nodes(mapped).reshape(owners, node_count // block_size, block_size, features)
    chosen = gathered[jnp.arange(owners), decode_block[:, 0]].reshape(owners * block_size, features)
    cells = decode_source.reshape(3, blocks, 2, part_rows)

    def outputs(half):
        indices = lax.dynamic_index_in_dim(cells, half, 2, keepdims=False).reshape(3, -1)
        ids = jnp.arange(owners * block_size, dtype=jnp.int32)[None, :]
        counts = sum((indices[e][:, None] == ids).astype(jnp.float32) for e in range(3))
        summed = jnp.dot(counts.astype(jnp.bfloat16), chosen, preferred_element_type=jnp.float32)
        hidden = jax.nn.silu(summed).astype(jnp.bfloat16)
        return jnp.dot(hidden, output_all, preferred_element_type=jnp.float32)

    leaving = outputs(1 - phase_index).astype(jnp.bfloat16)
    arriving = swap(leaving).astype(jnp.float32)
    kept = outputs(phase_index)
    skipped = jnp.einsum(
        "mgrd,do->mgro", grid_fields, skip_weight, preferred_element_type=jnp.float32
    )
    here = (jnp.arange(2) == phase_index)[:, None, None, None]
    shape = (1, blocks, part_rows, kept.shape[1])
    return jnp.where(here, kept.reshape(shape), arriving.reshape(shape)) + skipped


def on_device(grid_fields, *others):
    phases, batches = lax.axis_size("phase"), grid_fields.shape[0]
    owners = lax.axis_size("shard")
    if phases == batches == 2 and owners == DEPTH * ROWS * CORES and others[10].shape[2] == 1:
        return on_device_batches(grid_fields, *others)
    return on_device_sections(grid_fields, *others)


def solution(mesh):
    return jax.shard_map(
        on_device,
        mesh=mesh,
        in_specs=(
            P(None, "shard", "phase", None),
            P(),
            P("shard", None, None),
            P("shard", None),
            P("shard", None, None, None),
            P("phase", None, None),
            P("phase", None, None),
            P("phase", None),
            P("shard", None, None),
            P("shard", None),
            P(None, "phase"),
            P("shard", None, None),
            P(None, "shard"),
            P("phase", None),
            P(),
        ),
        out_specs=P(None, "shard", "phase", None),
        check_vma=False,
    )
```

```python
import math

import jax
import jax.numpy as jnp
from jax import lax
from jax.experimental import pallas as pl
from jax.experimental.pallas import tpu as pltpu
from jax.sharding import PartitionSpec as P


def from_behind(value, axis, by):
    length = lax.axis_size(axis)
    pairs = [(i, i + by) for i in range(length) if 0 <= i + by < length]
    return lax.ppermute(value, axis, pairs)


def broadcast(block, axis, source):
    block = jnp.where(lax.axis_index(axis) == source, block, jnp.zeros_like(block))
    return lax.psum(block, axis)


def layer_norm(values):
    average = jnp.mean(values, axis=-1, keepdims=True)
    centred = values - average
    variance = jnp.mean(centred * centred, axis=-1, keepdims=True)
    return centred * lax.rsqrt(variance + 1e-05)


def add_by_target(values, targets, node_count):
    row_count, columns = values.shape
    block_rows = math.gcd(row_count, 2048)
    value_blocks = values.reshape(row_count // block_rows, block_rows, columns)
    target_blocks = targets.reshape(row_count // block_rows, block_rows)
    node_ids = jnp.arange(node_count, dtype=jnp.int32)

    def accumulate(running, pieces):
        onehot = (pieces[1][None, :] == node_ids[:, None]).astype(jnp.bfloat16)
        return (running + jnp.dot(onehot, pieces[0], preferred_element_type=jnp.float32), None)

    running, unused = lax.scan(
        accumulate, jnp.zeros((node_count, columns), jnp.float32), (value_blocks, target_blocks)
    )
    return running


def encode_sums(messages, send_blocks, slot_live, targets, node_count):
    picked = messages[send_blocks]
    picked = jnp.where(slot_live[:, :, None, None, None], picked, jnp.zeros_like(picked))
    arrived = lax.all_to_all(picked, "shard", split_axis=0, concat_axis=0, tiled=True)
    peer_count, capacity, part_rows, batches, columns = arrived.shape
    node_ids = jnp.where(targets >= 0, targets, node_count).reshape(-1)
    summed = add_by_target(
        arrived.reshape(peer_count * capacity * part_rows, batches * columns), node_ids, node_count
    )
    return jnp.transpose(summed.reshape(node_count, batches, columns), (1, 0, 2))


def on_device_sections(
    grid_fields,
    encode_weight,
    encode_send,
    encode_count,
    encode_target,
    edge_weight,
    node_weight,
    node_gain,
    mesh_send,
    mesh_neighbour,
    decode_weight,
    decode_send,
    decode_source,
    output_weight,
    skip_weight,
):
    phases = lax.axis_size("phase")
    phase_index = lax.axis_index("phase")
    batches, blocks, part_rows, features = grid_fields.shape
    node_count = mesh_neighbour.shape[0]
    block_size = encode_target.shape[3]
    send_blocks = encode_send[0]
    capacity = send_blocks.shape[1]
    slot_live = jnp.arange(capacity, dtype=jnp.int32)[None, :] < encode_count[0][:, None]
    messages = jax.nn.silu(
        jnp.einsum("mgrd,dc->grmc", grid_fields, encode_weight, preferred_element_type=jnp.float32)
    ).astype(jnp.bfloat16)
    own_targets = lax.dynamic_slice_in_dim(encode_target[0], phase_index * part_rows, part_rows, 2)
    partial_sums = encode_sums(messages, send_blocks, slot_live, own_targets, node_count)
    encoded = lax.psum(partial_sums, "phase")
    initial = layer_norm(encoded).astype(jnp.bfloat16)
    my_edge = edge_weight[0]
    my_node = node_weight[0]
    my_gain = node_gain[0]
    send_nodes = mesh_send[0]
    edge_live = mesh_neighbour >= 0
    safe_index = jnp.where(edge_live, mesh_neighbour, 0)
    slot_count = mesh_neighbour.shape[1]

    def process(mesh_state):
        both_parts = jnp.dot(mesh_state, my_edge, preferred_element_type=jnp.float32)
        source_part = both_parts[:, :features].astype(jnp.bfloat16)
        dest_part = both_parts[:, features:]
        incoming = lax.all_to_all(
            source_part[send_nodes], "shard", split_axis=0, concat_axis=0, tiled=True
        )
        lookup_table = jnp.concatenate([source_part, incoming.reshape(-1, features)], axis=0)
        running = jnp.zeros((node_count, features), jnp.float32)
        for slot_index in range(slot_count):
            gathered = lookup_table[safe_index[:, slot_index]].astype(jnp.float32)
            running = running + jnp.where(
                edge_live[:, slot_index][:, None], jax.nn.silu(gathered + dest_part), 0.0
            )
        summary = running.astype(jnp.bfloat16)
        mixed = jnp.dot(mesh_state, my_node[:features], preferred_element_type=jnp.float32)
        mixed = mixed + jnp.dot(summary, my_node[features:], preferred_element_type=jnp.float32)
        return (mesh_state.astype(jnp.float32) + my_gain * layer_norm(jax.nn.silu(mixed))).astype(
            jnp.bfloat16
        )

    tick_count = batches + phases - 1

    def advance(carried, tick_index):
        current, finished = carried
        entering = lax.dynamic_index_in_dim(
            initial, jnp.minimum(tick_index, batches - 1), 0, keepdims=False
        )
        inputs = jnp.where(phase_index == 0, entering, current)
        result = process(inputs)
        leaving = tick_index - (phases - 1)
        updated = lax.dynamic_update_index_in_dim(finished, result, jnp.maximum(leaving, 0), 0)
        finished = jnp.where((phase_index == phases - 1) & (leaving >= 0), updated, finished)
        current = from_behind(result, "phase", 1)
        return ((current, finished), None)

    carried, unused = lax.scan(
        advance,
        (jnp.zeros_like(initial[0]), jnp.zeros_like(initial)),
        jnp.arange(tick_count, dtype=jnp.int32),
    )
    finished = carried[1]
    final_states = broadcast(finished, "phase", phases - 1)
    mapped = jnp.einsum(
        "mnd,dc->nmc", final_states, decode_weight, preferred_element_type=jnp.float32
    ).astype(jnp.bfloat16)
    columns = mapped.shape[2]
    node_blocks = mapped.reshape(node_count // block_size, block_size, batches, columns)
    outgoing = node_blocks[decode_send[0]]
    arrived = lax.all_to_all(outgoing, "shard", split_axis=0, concat_axis=0, tiled=True)
    arrived = arrived.reshape(-1, batches, columns)
    summed = arrived[decode_source[0]].astype(jnp.float32)
    summed = summed + arrived[decode_source[1]].astype(jnp.float32)
    summed = summed + arrived[decode_source[2]].astype(jnp.float32)
    hidden = jax.nn.silu(summed).astype(jnp.bfloat16)
    skipped = jnp.einsum(
        "mgrd,do->mgro", grid_fields, skip_weight, preferred_element_type=jnp.float32
    )
    output_terms = jnp.einsum(
        "rmc,co->mro", hidden, output_weight, preferred_element_type=jnp.float32
    )
    output_terms = output_terms.reshape(batches, blocks, block_size, output_terms.shape[2])
    shared = lax.psum_scatter(output_terms, "phase", scatter_dimension=2, tiled=True)
    return shared + skipped


def swap(value):
    return lax.ppermute(value, "phase", [(0, 1), (1, 0)])


MESH_ID = pl.DeviceIdType.MESH
PIECE = 128
DEPTH, ROWS, CORES = 4, 2, 2


def greet(peers):
    barrier = pltpu.get_barrier_semaphore()
    for peer in peers:
        pl.semaphore_signal(barrier, inc=1, device_id=peer, device_id_type=MESH_ID)
    pl.semaphore_wait(barrier, len(peers))


def send(source, target, sems, at, peer):
    copy = pltpu.make_async_remote_copy(
        src_ref=source,
        dst_ref=target,
        send_sem=sems.at[0, at],
        recv_sem=sems.at[1, at],
        device_id=peer,
        device_id_type=MESH_ID,
    )
    copy.start()
    return copy


def places():
    phase, me = lax.axis_index("phase"), lax.axis_index("shard")
    z, y, c = me // 4, (me // 2) % 2, me % 2

    def at(z, y, c):
        return (phase, z * 4 + y * 2 + c)

    across = at(z, y, 1 - c)
    beside = at(z, 1 - y, c)
    line = [at((z + k) % DEPTH, y, c) for k in range(1, DEPTH)]
    return phase, me, z, y, c, across, beside, line


def owner_kernel(
    part, edge, node, states, edges, nodes,
    core_in, y_out, y_in, z_out, z_in, total, core_sems, y_sems, z_sems, weight_sems,
):
    phase, me, z, y, c, across, beside, line = places()
    partner = (1 - phase, me)
    keeps = [
        pltpu.make_async_copy(edge, edges.at[phase], weight_sems.at[0, 4]),
        pltpu.make_async_copy(node, nodes.at[phase], weight_sems.at[1, 4]),
    ]
    for keep in keeps:
        keep.start()
    greet([across, beside, partner] + line)
    step = 32
    tiles = part.shape[3] // step
    order = (2, 1, 3, 0)
    spots = [(z + k) % DEPTH for k in range(DEPTH)]
    core_copies = {}
    for k in order:
        core_copies[k] = send(
            part.at[spots[k], :, 1 - c], core_in.at[spots[k]], core_sems, k, across
        )
    weight_copies = [
        send(edge.at[c], edges.at[phase, c], weight_sems, 0, partner),
        send(node.at[c], nodes.at[phase, c], weight_sems, 1, partner),
    ]

    def over_tiles(body):
        def run(t, carry):
            body(pl.ds(pl.multiple_of(t * step, step), step))
            return carry

        lax.fori_loop(0, tiles, run, 0)

    def pair(spot, row, at):
        return part[spot, row, c, at, :].astype(jnp.float32) + core_in[spot, row, at, :].astype(
            jnp.float32
        )

    y_copies = {}
    for k in order:
        core_copies[k].wait()
        spot = spots[k]

        def to_beside(at):
            y_out[k, at, :] = pair(spot, 1 - y, at).astype(jnp.bfloat16)

        over_tiles(to_beside)
        y_copies[k] = send(y_out.at[k], y_in.at[k], y_sems, k, beside)
    z_copies = []
    for k in order:
        y_copies[k].wait()
        spot = spots[k]

        def add_up(at):
            value = pair(spot, y, at) + y_in[k, at, :].astype(jnp.float32)
            if k == 0:
                total[at, :] = value
            else:
                z_out[k - 1, at, :] = value.astype(jnp.bfloat16)

        over_tiles(add_up)
        if k:
            z_copies.append(send(z_out.at[k - 1], z_in.at[k - 1], z_sems, k - 1, line[k - 1]))
    for copy in weight_copies:
        copy.wait()
    weight_copies = [
        send(edges.at[1 - phase, c], edges.at[1 - phase, c], weight_sems, 2, across),
        send(nodes.at[1 - phase, c], nodes.at[1 - phase, c], weight_sems, 3, across),
    ]
    for copy in z_copies:
        copy.wait()

    def finish(at):
        value = total[at, :]
        for k in range(DEPTH - 1):
            value = value + z_in[k, at, :].astype(jnp.float32)
        states[at, :] = layer_norm(value).astype(jnp.bfloat16)

    over_tiles(finish)
    for copy in weight_copies + keeps:
        copy.wait()


def states_and_weights(partial_sums, edge, node):
    owners, nodes, features = partial_sums.shape
    part = partial_sums.reshape(DEPTH, ROWS, CORES, nodes, features)
    edge_half = edge.reshape(2, edge.shape[0] // 2, edge.shape[1])
    node_half = node.reshape(2, node.shape[0] // 2, node.shape[1])
    kind = jnp.bfloat16
    states, edges, node_weights = pl.pallas_call(
        owner_kernel,
        out_shape=(
            jax.ShapeDtypeStruct((nodes, features), kind),
            jax.ShapeDtypeStruct((2,) + edge_half.shape, kind),
            jax.ShapeDtypeStruct((2,) + node_half.shape, kind),
        ),
        in_specs=[pl.BlockSpec(memory_space=pltpu.VMEM)] * 3,
        out_specs=[pl.BlockSpec(memory_space=pltpu.VMEM)] * 3,
        scratch_shapes=[
            pltpu.VMEM((DEPTH, ROWS, nodes, features), kind),
            pltpu.VMEM((DEPTH, nodes, features), kind),
            pltpu.VMEM((DEPTH, nodes, features), kind),
            pltpu.VMEM((DEPTH - 1, nodes, features), kind),
            pltpu.VMEM((DEPTH - 1, nodes, features), kind),
            pltpu.VMEM((nodes, features), jnp.float32),
            pltpu.SemaphoreType.DMA((2, DEPTH)),
            pltpu.SemaphoreType.DMA((2, DEPTH)),
            pltpu.SemaphoreType.DMA((2, DEPTH - 1)),
            pltpu.SemaphoreType.DMA((2, 5)),
        ],
        compiler_params=pltpu.CompilerParams(
            collective_id=0, has_side_effects=True, vmem_limit_bytes=40 * 2**20
        ),
        name="sum_to_owners",
    )(part, edge_half, node_half)
    return states, edges.reshape((2,) + edge.shape), node_weights.reshape((2,) + node.shape)


def gather_kernel(mine, everyone, own_sem, z_sems, y_sems, core_sems):
    phase, me, z, y, c, across, beside, line = places()
    greet([across, beside] + line)
    pieces = mine.shape[0] // PIECE
    whole = everyone.at[z, y, c]
    spans = [pl.ds(p * PIECE, PIECE) for p in range(pieces)]
    keep = pltpu.make_async_copy(mine, whole, own_sem.at[0])
    z_copies, y_copies, core_copies = {}, {}, []
    for p, span in enumerate(spans):
        own, here = mine.at[span], everyone.at[z, y, c, span]
        for k in (2, 1, 3):
            z_copies[p, k] = send(own, here, z_sems, p * 4 + k, line[k - 1])
        y_copies[p, 0] = send(own, here, y_sems, p * 4, beside)
        core_copies.append(send(own, here, core_sems, p * 8, across))
    keep.start()
    for p, span in enumerate(spans):
        for k in (1, 3, 2):
            z_copies[p, k].wait()
            block = everyone.at[(z + DEPTH - k) % DEPTH, y, c, span]
            y_copies[p, k] = send(block, block, y_sems, p * 4 + k, beside)
            core_copies.append(send(block, block, core_sems, p * 8 + k, across))
    for p, span in enumerate(spans):
        for k in (0, 1, 3, 2):
            y_copies[p, k].wait()
            block = everyone.at[(z + DEPTH - k) % DEPTH, 1 - y, c, span]
            core_copies.append(send(block, block, core_sems, p * 8 + 4 + k, across))
    keep.wait()
    for copy in core_copies:
        copy.wait()


def gather_nodes(mapped):
    pieces = mapped.shape[0] // PIECE
    return pl.pallas_call(
        gather_kernel,
        out_shape=jax.ShapeDtypeStruct((DEPTH, ROWS, CORES) + mapped.shape, mapped.dtype),
        in_specs=[pl.BlockSpec(memory_space=pltpu.VMEM)],
        out_specs=pl.BlockSpec(memory_space=pltpu.VMEM),
        scratch_shapes=[
            pltpu.SemaphoreType.DMA((1,)),
            pltpu.SemaphoreType.DMA((2, 4 * pieces)),
            pltpu.SemaphoreType.DMA((2, 4 * pieces)),
            pltpu.SemaphoreType.DMA((2, 8 * pieces)),
        ],
        compiler_params=pltpu.CompilerParams(
            collective_id=1, has_side_effects=True, vmem_limit_bytes=24 * 2**20
        ),
        name="gather_nodes",
    )(mapped)


def silu(values):
    half = 0.5 * values
    return half + half * jnp.tanh(half)


def sections_kernel(
    first, edges, nodes, gains, source_hot, live, send_hot, decode, mapped,
    states, outgoing, incoming, table, dest, mixed, running, send_sems, recv_sems,
):
    phase, me = lax.axis_index("phase"), lax.axis_index("shard")
    owners, lanes = incoming.shape[1], incoming.shape[3]
    node_count, features = first.shape
    slots = source_hot.shape[0]
    peers = [lax.rem(me + k, owners) for k in range(1, owners)]
    greet([(phase, peer) for peer in peers])
    packed = owners * 16
    chunk_of_row = (lax.broadcasted_iota(jnp.int32, (packed, lanes), 0) // 4) % 4
    states[...] = first[...]

    def dot(left, right):
        return jnp.dot(left, right, preferred_element_type=jnp.float32)

    for layer in range(2):
        source = dot(states[...], edges[layer, :, :features]).astype(jnp.bfloat16)
        table[:node_count, :] = source
        chosen = dot(send_hot[...], source)
        payload = jnp.zeros((packed, lanes), jnp.float32)
        for j in range(4):
            payload = jnp.where(chunk_of_row == j, chosen[:, j * lanes : (j + 1) * lanes], payload)
        outgoing[layer] = payload.astype(jnp.bfloat16).reshape(owners, 16, lanes)
        copies = []
        for k, peer in enumerate(peers):
            copy = pltpu.make_async_remote_copy(
                src_ref=outgoing.at[layer, peer],
                dst_ref=incoming.at[layer, me],
                send_sem=send_sems.at[layer, k],
                recv_sem=recv_sems.at[layer, k],
                device_id=(phase, peer),
                device_id_type=MESH_ID,
            )
            copy.start()
            copies.append(copy)
        incoming[layer, me] = outgoing[layer, me]
        dest[...] = dot(states[...], edges[layer, :, features:])
        mixed[...] = dot(states[...], nodes[layer, :features, :])
        running[...] = jnp.zeros_like(running)
        for copy in copies:
            copy.wait()
        arrived = incoming[layer].reshape(packed, lanes).astype(jnp.float32)
        for j in range(4):
            table[node_count:, j * lanes : (j + 1) * lanes] = jnp.where(
                chunk_of_row == j, arrived, 0.0
            ).astype(jnp.bfloat16)

        def one_slot(slot, carry):
            gathered = dot(source_hot[slot], table[...])
            running[...] += silu(gathered + dest[...]) * live[slot]
            return carry

        lax.fori_loop(0, slots, one_slot, 0)
        value = mixed[...] + dot(running[...].astype(jnp.bfloat16), nodes[layer, features:, :])
        value = gains[layer] * layer_norm(silu(value))
        states[...] = (states[...].astype(jnp.float32) + value).astype(jnp.bfloat16)
    mapped[...] = dot(states[...], decode[...]).astype(jnp.bfloat16)


def run_sections(states, edges, nodes, gains, source_hot, live, send_hot, decode, owners):
    node_count, features = states.shape
    lanes = features // 4
    kind = jnp.bfloat16
    return pl.pallas_call(
        sections_kernel,
        out_shape=jax.ShapeDtypeStruct((node_count, features), kind),
        in_specs=[pl.BlockSpec(memory_space=pltpu.VMEM)] * 8,
        out_specs=pl.BlockSpec(memory_space=pltpu.VMEM),
        scratch_shapes=[
            pltpu.VMEM((node_count, features), kind),
            pltpu.VMEM((2, owners, 16, lanes), kind),
            pltpu.VMEM((2, owners, 16, lanes), kind),
            pltpu.VMEM((node_count + owners * 16, features), kind),
            pltpu.VMEM((node_count, features), jnp.float32),
            pltpu.VMEM((node_count, features), jnp.float32),
            pltpu.VMEM((node_count, features), jnp.float32),
            pltpu.SemaphoreType.DMA((2, owners - 1)),
            pltpu.SemaphoreType.DMA((2, owners - 1)),
        ],
        compiler_params=pltpu.CompilerParams(
            collective_id=2, has_side_effects=True, vmem_limit_bytes=40 * 2**20
        ),
        name="run_sections",
    )(states, edges, nodes, gains, source_hot, live, send_hot, decode)


def on_device_batches(
    grid_fields,
    encode_weight,
    encode_send,
    encode_count,
    encode_target,
    edge_weight,
    node_weight,
    node_gain,
    mesh_send,
    mesh_neighbour,
    decode_weight,
    decode_send,
    decode_source,
    output_weight,
    skip_weight,
):
    phase_index = lax.axis_index("phase")
    owners = lax.axis_size("shard")
    batches, blocks, part_rows, features = grid_fields.shape
    node_count, slot_count = mesh_neighbour.shape
    block_size = encode_target.shape[3]
    send_blocks = encode_send[0]
    capacity = send_blocks.shape[1]

    messages = jax.nn.silu(
        jnp.einsum("mgrd,dc->mgrc", grid_fields, encode_weight, preferred_element_type=jnp.float32)
    ).astype(jnp.bfloat16)
    own = lax.dynamic_index_in_dim(messages, phase_index, 0, keepdims=False)
    away = lax.dynamic_index_in_dim(messages, 1 - phase_index, 0, keepdims=False)
    came = swap(away)
    rows = jnp.concatenate([own, came], axis=1)

    tables = jnp.concatenate(
        [encode_target[0].reshape(owners, -1), decode_send[0].reshape(owners, -1)], axis=1
    )
    tables = lax.all_to_all(tables, "shard", split_axis=0, concat_axis=0, tiled=True)
    targets = tables[:, : capacity * block_size].reshape(owners, capacity, 2, part_rows)
    decode_block = tables[:, capacity * block_size :]
    targets = jnp.where(phase_index == 0, targets, targets[:, :, ::-1])
    targets = targets.reshape(owners, capacity * block_size)
    slot_live = jnp.arange(capacity, dtype=jnp.int32)[None, :] < encode_count[0][:, None]
    live = jnp.repeat(slot_live, block_size, axis=1)
    targets = jnp.where(live, targets, -1)
    hot = targets[:, None, :] == jnp.arange(node_count, dtype=jnp.int32)[None, :, None]
    picked = rows[send_blocks].reshape(owners, capacity * block_size, features)
    partial_sums = jnp.einsum(
        "onr,orc->onc", hot.astype(jnp.bfloat16), picked, preferred_element_type=jnp.float32
    ).astype(jnp.bfloat16)
    states, edges, nodes = states_and_weights(partial_sums, edge_weight[0], node_weight[0])
    other_gain = swap(node_gain[0])
    first = phase_index == 0
    gains = jnp.stack(
        [jnp.where(first, node_gain[0], other_gain), jnp.where(first, other_gain, node_gain[0])]
    )[:, None, :]
    decode_all = jnp.concatenate([decode_weight, swap(decode_weight)], axis=1)
    output_all = jnp.concatenate([output_weight, swap(output_weight)], axis=0)

    neighbour = mesh_neighbour.T
    packed = jnp.arange(owners * 16, dtype=jnp.int32)
    columns = jnp.concatenate(
        [jnp.arange(node_count, dtype=jnp.int32), node_count + packed // 16 * 4 + packed % 4]
    )
    source_hot = (neighbour[:, :, None] == columns).astype(jnp.bfloat16)
    live = (neighbour >= 0).astype(jnp.float32)[:, :, None]
    send_nodes = jnp.tile(mesh_send[0][:, None, :], (1, 4, 1)).reshape(-1)
    send_hot = send_nodes[:, None] == jnp.arange(node_count, dtype=jnp.int32)
    mapped = run_sections(
        states, edges, nodes, gains, source_hot, live, send_hot.astype(jnp.bfloat16), decode_all, owners
    )

    gathered = gather_nodes(mapped).reshape(owners, node_count // block_size, block_size, features)
    chosen = gathered[jnp.arange(owners), decode_block[:, 0]].reshape(owners * block_size, features)
    cells = decode_source.reshape(3, blocks, 2, part_rows)

    def outputs(half):
        indices = lax.dynamic_index_in_dim(cells, half, 2, keepdims=False).reshape(3, -1)
        ids = jnp.arange(owners * block_size, dtype=jnp.int32)[None, :]
        counts = sum((indices[e][:, None] == ids).astype(jnp.float32) for e in range(3))
        summed = jnp.dot(counts.astype(jnp.bfloat16), chosen, preferred_element_type=jnp.float32)
        hidden = jax.nn.silu(summed).astype(jnp.bfloat16)
        return jnp.dot(hidden, output_all, preferred_element_type=jnp.float32)

    leaving = outputs(1 - phase_index).astype(jnp.bfloat16)
    arriving = swap(leaving).astype(jnp.float32)
    kept = outputs(phase_index)
    skipped = jnp.einsum(
        "mgrd,do->mgro", grid_fields, skip_weight, preferred_element_type=jnp.float32
    )
    here = (jnp.arange(2) == phase_index)[:, None, None, None]
    shape = (1, blocks, part_rows, kept.shape[1])
    return jnp.where(here, kept.reshape(shape), arriving.reshape(shape)) + skipped


def on_device(grid_fields, *others):
    phases, batches = lax.axis_size("phase"), grid_fields.shape[0]
    owners = lax.axis_size("shard")
    if phases == batches == 2 and owners == DEPTH * ROWS * CORES and others[7].shape[2] == 4 and others[10].shape[2] == 1:
        return on_device_batches(grid_fields, *others)
    return on_device_sections(grid_fields, *others)


def solution(mesh):
    return jax.shard_map(
        on_device,
        mesh=mesh,
        in_specs=(
            P(None, "shard", "phase", None),
            P(),
            P("shard", None, None),
            P("shard", None),
            P("shard", None, None, None),
            P("phase", None, None),
            P("phase", None, None),
            P("phase", None),
            P("shard", None, None),
            P("shard", None),
            P(None, "phase"),
            P("shard", None, None),
            P(None, "shard"),
            P("phase", None),
            P(),
        ),
        out_specs=P(None, "shard", "phase", None),
        check_vma=False,
    )
```

```python
import math

import jax
import jax.numpy as jnp
from jax import lax
from jax.experimental import pallas as pl
from jax.experimental.pallas import tpu as pltpu
from jax.sharding import PartitionSpec as P


def from_behind(value, axis, by):
    length = lax.axis_size(axis)
    pairs = [(i, i + by) for i in range(length) if 0 <= i + by < length]
    return lax.ppermute(value, axis, pairs)


def broadcast(block, axis, source):
    block = jnp.where(lax.axis_index(axis) == source, block, jnp.zeros_like(block))
    return lax.psum(block, axis)


def layer_norm(values):
    average = jnp.mean(values, axis=-1, keepdims=True)
    centred = values - average
    variance = jnp.mean(centred * centred, axis=-1, keepdims=True)
    return centred * lax.rsqrt(variance + 1e-05)


def add_by_target(values, targets, node_count):
    row_count, columns = values.shape
    block_rows = math.gcd(row_count, 2048)
    value_blocks = values.reshape(row_count // block_rows, block_rows, columns)
    target_blocks = targets.reshape(row_count // block_rows, block_rows)
    node_ids = jnp.arange(node_count, dtype=jnp.int32)

    def accumulate(running, pieces):
        onehot = (pieces[1][None, :] == node_ids[:, None]).astype(jnp.bfloat16)
        return (running + jnp.dot(onehot, pieces[0], preferred_element_type=jnp.float32), None)

    running, unused = lax.scan(
        accumulate, jnp.zeros((node_count, columns), jnp.float32), (value_blocks, target_blocks)
    )
    return running


def encode_sums(messages, send_blocks, slot_live, targets, node_count):
    picked = messages[send_blocks]
    picked = jnp.where(slot_live[:, :, None, None, None], picked, jnp.zeros_like(picked))
    arrived = lax.all_to_all(picked, "shard", split_axis=0, concat_axis=0, tiled=True)
    peer_count, capacity, part_rows, batches, columns = arrived.shape
    node_ids = jnp.where(targets >= 0, targets, node_count).reshape(-1)
    summed = add_by_target(
        arrived.reshape(peer_count * capacity * part_rows, batches * columns), node_ids, node_count
    )
    return jnp.transpose(summed.reshape(node_count, batches, columns), (1, 0, 2))


def on_device_sections(
    grid_fields,
    encode_weight,
    encode_send,
    encode_count,
    encode_target,
    edge_weight,
    node_weight,
    node_gain,
    mesh_send,
    mesh_neighbour,
    decode_weight,
    decode_send,
    decode_source,
    output_weight,
    skip_weight,
):
    phases = lax.axis_size("phase")
    phase_index = lax.axis_index("phase")
    batches, blocks, part_rows, features = grid_fields.shape
    node_count = mesh_neighbour.shape[0]
    block_size = encode_target.shape[3]
    send_blocks = encode_send[0]
    capacity = send_blocks.shape[1]
    slot_live = jnp.arange(capacity, dtype=jnp.int32)[None, :] < encode_count[0][:, None]
    messages = jax.nn.silu(
        jnp.einsum("mgrd,dc->grmc", grid_fields, encode_weight, preferred_element_type=jnp.float32)
    ).astype(jnp.bfloat16)
    own_targets = lax.dynamic_slice_in_dim(encode_target[0], phase_index * part_rows, part_rows, 2)
    partial_sums = encode_sums(messages, send_blocks, slot_live, own_targets, node_count)
    encoded = lax.psum(partial_sums, "phase")
    initial = layer_norm(encoded).astype(jnp.bfloat16)
    my_edge = edge_weight[0]
    my_node = node_weight[0]
    my_gain = node_gain[0]
    send_nodes = mesh_send[0]
    edge_live = mesh_neighbour >= 0
    safe_index = jnp.where(edge_live, mesh_neighbour, 0)
    slot_count = mesh_neighbour.shape[1]

    def process(mesh_state):
        both_parts = jnp.dot(mesh_state, my_edge, preferred_element_type=jnp.float32)
        source_part = both_parts[:, :features].astype(jnp.bfloat16)
        dest_part = both_parts[:, features:]
        incoming = lax.all_to_all(
            source_part[send_nodes], "shard", split_axis=0, concat_axis=0, tiled=True
        )
        lookup_table = jnp.concatenate([source_part, incoming.reshape(-1, features)], axis=0)
        running = jnp.zeros((node_count, features), jnp.float32)
        for slot_index in range(slot_count):
            gathered = lookup_table[safe_index[:, slot_index]].astype(jnp.float32)
            running = running + jnp.where(
                edge_live[:, slot_index][:, None], jax.nn.silu(gathered + dest_part), 0.0
            )
        summary = running.astype(jnp.bfloat16)
        mixed = jnp.dot(mesh_state, my_node[:features], preferred_element_type=jnp.float32)
        mixed = mixed + jnp.dot(summary, my_node[features:], preferred_element_type=jnp.float32)
        return (mesh_state.astype(jnp.float32) + my_gain * layer_norm(jax.nn.silu(mixed))).astype(
            jnp.bfloat16
        )

    tick_count = batches + phases - 1

    def advance(carried, tick_index):
        current, finished = carried
        entering = lax.dynamic_index_in_dim(
            initial, jnp.minimum(tick_index, batches - 1), 0, keepdims=False
        )
        inputs = jnp.where(phase_index == 0, entering, current)
        result = process(inputs)
        leaving = tick_index - (phases - 1)
        updated = lax.dynamic_update_index_in_dim(finished, result, jnp.maximum(leaving, 0), 0)
        finished = jnp.where((phase_index == phases - 1) & (leaving >= 0), updated, finished)
        current = from_behind(result, "phase", 1)
        return ((current, finished), None)

    carried, unused = lax.scan(
        advance,
        (jnp.zeros_like(initial[0]), jnp.zeros_like(initial)),
        jnp.arange(tick_count, dtype=jnp.int32),
    )
    finished = carried[1]
    final_states = broadcast(finished, "phase", phases - 1)
    mapped = jnp.einsum(
        "mnd,dc->nmc", final_states, decode_weight, preferred_element_type=jnp.float32
    ).astype(jnp.bfloat16)
    columns = mapped.shape[2]
    node_blocks = mapped.reshape(node_count // block_size, block_size, batches, columns)
    outgoing = node_blocks[decode_send[0]]
    arrived = lax.all_to_all(outgoing, "shard", split_axis=0, concat_axis=0, tiled=True)
    arrived = arrived.reshape(-1, batches, columns)
    summed = arrived[decode_source[0]].astype(jnp.float32)
    summed = summed + arrived[decode_source[1]].astype(jnp.float32)
    summed = summed + arrived[decode_source[2]].astype(jnp.float32)
    hidden = jax.nn.silu(summed).astype(jnp.bfloat16)
    skipped = jnp.einsum(
        "mgrd,do->mgro", grid_fields, skip_weight, preferred_element_type=jnp.float32
    )
    output_terms = jnp.einsum(
        "rmc,co->mro", hidden, output_weight, preferred_element_type=jnp.float32
    )
    output_terms = output_terms.reshape(batches, blocks, block_size, output_terms.shape[2])
    shared = lax.psum_scatter(output_terms, "phase", scatter_dimension=2, tiled=True)
    return shared + skipped


def swap(value):
    return lax.ppermute(value, "phase", [(0, 1), (1, 0)])


MESH_ID = pl.DeviceIdType.MESH
PIECE = 128
DEPTH, ROWS, CORES = 4, 2, 2


def greet(peers):
    barrier = pltpu.get_barrier_semaphore()
    for peer in peers:
        pl.semaphore_signal(barrier, inc=1, device_id=peer, device_id_type=MESH_ID)
    pl.semaphore_wait(barrier, len(peers))


def send(source, target, sems, at, peer):
    copy = pltpu.make_async_remote_copy(
        src_ref=source,
        dst_ref=target,
        send_sem=sems.at[0, at],
        recv_sem=sems.at[1, at],
        device_id=peer,
        device_id_type=MESH_ID,
    )
    copy.start()
    return copy


def places():
    phase, me = lax.axis_index("phase"), lax.axis_index("shard")
    z, y, c = me // 4, (me // 2) % 2, me % 2

    def at(z, y, c):
        return (phase, z * 4 + y * 2 + c)

    across = at(z, y, 1 - c)
    beside = at(z, 1 - y, c)
    line = [at((z + k) % DEPTH, y, c) for k in range(1, DEPTH)]
    return phase, me, z, y, c, across, beside, line


def owner_kernel(
    part, edge, node, decode, gain, states, edges, nodes, decode_other, gains,
    core_in, y_out, y_in, z_out, z_in, total, core_sems, y_sems, z_sems, weight_sems,
):
    phase, me, z, y, c, across, beside, line = places()
    partner = (1 - phase, me)
    keeps = [
        pltpu.make_async_copy(edge, edges.at[phase], weight_sems.at[0, 4]),
        pltpu.make_async_copy(node, nodes.at[phase], weight_sems.at[1, 4]),
        pltpu.make_async_copy(gain, gains.at[phase], weight_sems.at[0, 7]),
    ]
    for keep in keeps:
        keep.start()
    greet([across, beside, partner] + line)
    step = 32
    tiles = part.shape[3] // step
    order = (2, 1, 3, 0)
    spots = [(z + k) % DEPTH for k in range(DEPTH)]
    core_copies = {}
    for k in order:
        core_copies[k] = send(
            part.at[spots[k], :, 1 - c], core_in.at[spots[k]], core_sems, k, across
        )
    weight_copies = [
        send(edge.at[c], edges.at[phase, c], weight_sems, 0, partner),
        send(node.at[c], nodes.at[phase, c], weight_sems, 1, partner),
        send(decode, decode_other, weight_sems, 5, partner),
        send(gain, gains.at[phase], weight_sems, 6, partner),
    ]

    def over_tiles(body):
        def run(t, carry):
            body(pl.ds(pl.multiple_of(t * step, step), step))
            return carry

        lax.fori_loop(0, tiles, run, 0)

    def pair(spot, row, at):
        return part[spot, row, c, at, :].astype(jnp.float32) + core_in[spot, row, at, :].astype(
            jnp.float32
        )

    y_copies = {}
    for k in order:
        core_copies[k].wait()
        spot = spots[k]

        def to_beside(at):
            y_out[k, at, :] = pair(spot, 1 - y, at).astype(jnp.bfloat16)

        over_tiles(to_beside)
        y_copies[k] = send(y_out.at[k], y_in.at[k], y_sems, k, beside)
    z_copies = []
    for k in order:
        y_copies[k].wait()
        spot = spots[k]

        def add_up(at):
            value = pair(spot, y, at) + y_in[k, at, :].astype(jnp.float32)
            if k == 0:
                total[at, :] = value
            else:
                z_out[k - 1, at, :] = value.astype(jnp.bfloat16)

        over_tiles(add_up)
        if k:
            z_copies.append(send(z_out.at[k - 1], z_in.at[k - 1], z_sems, k - 1, line[k - 1]))
    for copy in weight_copies:
        copy.wait()
    weight_copies = [
        send(edges.at[1 - phase, c], edges.at[1 - phase, c], weight_sems, 2, across),
        send(nodes.at[1 - phase, c], nodes.at[1 - phase, c], weight_sems, 3, across),
    ]
    for copy in z_copies:
        copy.wait()

    def finish(at):
        value = total[at, :]
        for k in range(DEPTH - 1):
            value = value + z_in[k, at, :].astype(jnp.float32)
        states[at, :] = layer_norm(value).astype(jnp.bfloat16)

    over_tiles(finish)
    for copy in weight_copies + keeps:
        copy.wait()


def states_and_weights(partial_sums, edge, node, decode, gain):
    owners, nodes, features = partial_sums.shape
    part = partial_sums.reshape(DEPTH, ROWS, CORES, nodes, features)
    edge_half = edge.reshape(2, edge.shape[0] // 2, edge.shape[1])
    node_half = node.reshape(2, node.shape[0] // 2, node.shape[1])
    kind = jnp.bfloat16
    states, edges, node_weights, decode_other, gains = pl.pallas_call(
        owner_kernel,
        out_shape=(
            jax.ShapeDtypeStruct((nodes, features), kind),
            jax.ShapeDtypeStruct((2,) + edge_half.shape, kind),
            jax.ShapeDtypeStruct((2,) + node_half.shape, kind),
            jax.ShapeDtypeStruct(decode.shape, kind),
            jax.ShapeDtypeStruct((2,) + gain.shape, gain.dtype),
        ),
        in_specs=[pl.BlockSpec(memory_space=pltpu.VMEM)] * 5,
        out_specs=[pl.BlockSpec(memory_space=pltpu.VMEM)] * 5,
        scratch_shapes=[
            pltpu.VMEM((DEPTH, ROWS, nodes, features), kind),
            pltpu.VMEM((DEPTH, nodes, features), kind),
            pltpu.VMEM((DEPTH, nodes, features), kind),
            pltpu.VMEM((DEPTH - 1, nodes, features), kind),
            pltpu.VMEM((DEPTH - 1, nodes, features), kind),
            pltpu.VMEM((nodes, features), jnp.float32),
            pltpu.SemaphoreType.DMA((2, DEPTH)),
            pltpu.SemaphoreType.DMA((2, DEPTH)),
            pltpu.SemaphoreType.DMA((2, DEPTH - 1)),
            pltpu.SemaphoreType.DMA((2, 8)),
        ],
        compiler_params=pltpu.CompilerParams(
            collective_id=0, has_side_effects=True, vmem_limit_bytes=40 * 2**20
        ),
        name="sum_to_owners",
    )(part, edge_half, node_half, decode, gain)
    edges, node_weights = edges.reshape((2,) + edge.shape), node_weights.reshape((2,) + node.shape)
    return states, edges, node_weights, decode_other, gains


def gather_kernel(mine, everyone, own_sem, z_sems, y_sems, core_sems):
    phase, me, z, y, c, across, beside, line = places()
    greet([across, beside] + line)
    pieces = mine.shape[0] // PIECE
    whole = everyone.at[z, y, c]
    spans = [pl.ds(p * PIECE, PIECE) for p in range(pieces)]
    keep = pltpu.make_async_copy(mine, whole, own_sem.at[0])
    z_copies, y_copies, core_copies = {}, {}, []
    for p, span in enumerate(spans):
        own, here = mine.at[span], everyone.at[z, y, c, span]
        for k in (2, 1, 3):
            z_copies[p, k] = send(own, here, z_sems, p * 4 + k, line[k - 1])
        y_copies[p, 0] = send(own, here, y_sems, p * 4, beside)
        core_copies.append(send(own, here, core_sems, p * 8, across))
    keep.start()
    for p, span in enumerate(spans):
        for k in (1, 3, 2):
            z_copies[p, k].wait()
            block = everyone.at[(z + DEPTH - k) % DEPTH, y, c, span]
            y_copies[p, k] = send(block, block, y_sems, p * 4 + k, beside)
            core_copies.append(send(block, block, core_sems, p * 8 + k, across))
    for p, span in enumerate(spans):
        for k in (0, 1, 3, 2):
            y_copies[p, k].wait()
            block = everyone.at[(z + DEPTH - k) % DEPTH, 1 - y, c, span]
            core_copies.append(send(block, block, core_sems, p * 8 + 4 + k, across))
    keep.wait()
    for copy in core_copies:
        copy.wait()


def gather_nodes(mapped):
    pieces = mapped.shape[0] // PIECE
    return pl.pallas_call(
        gather_kernel,
        out_shape=jax.ShapeDtypeStruct((DEPTH, ROWS, CORES) + mapped.shape, mapped.dtype),
        in_specs=[pl.BlockSpec(memory_space=pltpu.VMEM)],
        out_specs=pl.BlockSpec(memory_space=pltpu.VMEM),
        scratch_shapes=[
            pltpu.SemaphoreType.DMA((1,)),
            pltpu.SemaphoreType.DMA((2, 4 * pieces)),
            pltpu.SemaphoreType.DMA((2, 4 * pieces)),
            pltpu.SemaphoreType.DMA((2, 8 * pieces)),
        ],
        compiler_params=pltpu.CompilerParams(
            collective_id=1, has_side_effects=True, vmem_limit_bytes=24 * 2**20
        ),
        name="gather_nodes",
    )(mapped)


def sum_rows_kernel(send_blocks, rows, targets, sums):
    owner = pl.program_id(0)
    block_size = rows.shape[1]
    nodes = lax.broadcasted_iota(jnp.int32, (sums.shape[1], block_size), 0)
    total = jnp.zeros(sums.shape[1:], jnp.float32)
    for slot in range(targets.shape[2] // block_size):
        wanted = targets[0, :, slot * block_size : (slot + 1) * block_size]
        hot = (nodes == wanted).astype(jnp.float32).astype(jnp.bfloat16)
        block = rows[send_blocks[owner, slot]]
        total = total + jnp.dot(hot, block, preferred_element_type=jnp.float32)
    sums[0] = total.astype(jnp.bfloat16)


def sum_rows(rows, send_blocks, targets, node_count):
    owners, width = targets.shape
    features = rows.shape[2]
    return pl.pallas_call(
        sum_rows_kernel,
        out_shape=jax.ShapeDtypeStruct((owners, node_count, features), jnp.bfloat16),
        grid_spec=pltpu.PrefetchScalarGridSpec(
            num_scalar_prefetch=1,
            grid=(owners,),
            in_specs=[
                pl.BlockSpec(rows.shape, lambda o, blocks: (0, 0, 0)),
                pl.BlockSpec((1, 1, width), lambda o, blocks: (o, 0, 0)),
            ],
            out_specs=pl.BlockSpec((1, node_count, features), lambda o, blocks: (o, 0, 0)),
        ),
        compiler_params=pltpu.CompilerParams(vmem_limit_bytes=24 * 2**20),
        name="sum_rows",
    )(send_blocks, rows, targets[:, None, :])


def silu(values):
    half = 0.5 * values
    return half + half * jnp.tanh(half)


def sections_kernel(
    first, edges, nodes, gains, source_hot, live, send_hot, decode, decode_other, mapped,
    states, outgoing, incoming, table, dest, mixed, running, send_sems, recv_sems,
):
    phase, me = lax.axis_index("phase"), lax.axis_index("shard")
    owners, lanes = incoming.shape[1], incoming.shape[3]
    node_count, features = first.shape
    slots = source_hot.shape[0]
    peers = [lax.rem(me + k, owners) for k in range(1, owners)]
    greet([(phase, peer) for peer in peers])
    packed = owners * 16
    chunk_of_row = (lax.broadcasted_iota(jnp.int32, (packed, lanes), 0) // 4) % 4
    states[...] = first[...]

    def dot(left, right):
        return jnp.dot(left, right, preferred_element_type=jnp.float32)

    for layer in range(2):
        source = dot(states[...], edges[layer, :, :features]).astype(jnp.bfloat16)
        table[:node_count, :] = source
        chosen = dot(send_hot[...], source)
        payload = jnp.zeros((packed, lanes), jnp.float32)
        for j in range(4):
            payload = jnp.where(chunk_of_row == j, chosen[:, j * lanes : (j + 1) * lanes], payload)
        outgoing[layer] = payload.astype(jnp.bfloat16).reshape(owners, 16, lanes)
        copies = []
        for k, peer in enumerate(peers):
            copy = pltpu.make_async_remote_copy(
                src_ref=outgoing.at[layer, peer],
                dst_ref=incoming.at[layer, me],
                send_sem=send_sems.at[layer, k],
                recv_sem=recv_sems.at[layer, k],
                device_id=(phase, peer),
                device_id_type=MESH_ID,
            )
            copy.start()
            copies.append(copy)
        incoming[layer, me] = outgoing[layer, me]
        dest[...] = dot(states[...], edges[layer, :, features:])
        mixed[...] = dot(states[...], nodes[layer, :features, :])
        running[...] = jnp.zeros_like(running)
        for copy in copies:
            copy.wait()
        arrived = incoming[layer].reshape(packed, lanes).astype(jnp.float32)
        for j in range(4):
            table[node_count:, j * lanes : (j + 1) * lanes] = jnp.where(
                chunk_of_row == j, arrived, 0.0
            ).astype(jnp.bfloat16)

        def one_slot(slot, carry):
            gathered = dot(source_hot[slot], table[...])
            running[...] += silu(gathered + dest[...]) * live[slot]
            return carry

        lax.fori_loop(0, slots, one_slot, 0)
        value = mixed[...] + dot(running[...].astype(jnp.bfloat16), nodes[layer, features:, :])
        value = gains[layer] * layer_norm(silu(value))
        states[...] = (states[...].astype(jnp.float32) + value).astype(jnp.bfloat16)
    width = decode.shape[1]
    mapped[:, :width] = dot(states[...], decode[...]).astype(jnp.bfloat16)
    mapped[:, width:] = dot(states[...], decode_other[...]).astype(jnp.bfloat16)


def run_sections(
    states, edges, nodes, gains, source_hot, live, send_hot, decode, decode_other, owners
):
    node_count, features = states.shape
    lanes = features // 4
    kind = jnp.bfloat16
    return pl.pallas_call(
        sections_kernel,
        out_shape=jax.ShapeDtypeStruct((node_count, features), kind),
        in_specs=[pl.BlockSpec(memory_space=pltpu.VMEM)] * 9,
        out_specs=pl.BlockSpec(memory_space=pltpu.VMEM),
        scratch_shapes=[
            pltpu.VMEM((node_count, features), kind),
            pltpu.VMEM((2, owners, 16, lanes), kind),
            pltpu.VMEM((2, owners, 16, lanes), kind),
            pltpu.VMEM((node_count + owners * 16, features), kind),
            pltpu.VMEM((node_count, features), jnp.float32),
            pltpu.VMEM((node_count, features), jnp.float32),
            pltpu.VMEM((node_count, features), jnp.float32),
            pltpu.SemaphoreType.DMA((2, owners - 1)),
            pltpu.SemaphoreType.DMA((2, owners - 1)),
        ],
        compiler_params=pltpu.CompilerParams(
            collective_id=2, has_side_effects=True, vmem_limit_bytes=40 * 2**20
        ),
        name="run_sections",
    )(states, edges, nodes, gains, source_hot, live, send_hot, decode, decode_other)


def on_device_batches(
    grid_fields,
    encode_weight,
    encode_send,
    encode_count,
    encode_target,
    edge_weight,
    node_weight,
    node_gain,
    mesh_send,
    mesh_neighbour,
    decode_weight,
    decode_send,
    decode_source,
    output_weight,
    skip_weight,
):
    phase_index = lax.axis_index("phase")
    owners = lax.axis_size("shard")
    batches, blocks, part_rows, features = grid_fields.shape
    node_count, slot_count = mesh_neighbour.shape
    block_size = encode_target.shape[3]
    send_blocks = encode_send[0]
    capacity = send_blocks.shape[1]

    messages = jax.nn.silu(
        jnp.einsum("mgrd,dc->mgrc", grid_fields, encode_weight, preferred_element_type=jnp.float32)
    ).astype(jnp.bfloat16)
    own = lax.dynamic_index_in_dim(messages, phase_index, 0, keepdims=False)
    away = lax.dynamic_index_in_dim(messages, 1 - phase_index, 0, keepdims=False)
    came = swap(away)
    rows = jnp.concatenate([own, came], axis=1)

    tables = jnp.concatenate(
        [encode_target[0].reshape(owners, -1), decode_send[0].reshape(owners, -1)], axis=1
    )
    tables = lax.all_to_all(tables, "shard", split_axis=0, concat_axis=0, tiled=True)
    targets = tables[:, : capacity * block_size].reshape(owners, capacity, 2, part_rows)
    decode_block = tables[:, capacity * block_size :]
    targets = jnp.where(phase_index == 0, targets, targets[:, :, ::-1])
    targets = targets.reshape(owners, capacity * block_size)
    slot_live = jnp.arange(capacity, dtype=jnp.int32)[None, :] < encode_count[0][:, None]
    live = jnp.repeat(slot_live, block_size, axis=1)
    targets = jnp.where(live, targets, -1)
    partial_sums = sum_rows(rows, send_blocks, targets, node_count)

    states, edges, nodes, decode_other, gains = states_and_weights(
        partial_sums, edge_weight[0], node_weight[0], decode_weight, node_gain
    )
    states, output_weight = lax.optimization_barrier((states, output_weight))
    output_all = jnp.concatenate([output_weight, swap(output_weight)], axis=0)

    neighbour = mesh_neighbour.T
    packed = jnp.arange(owners * 16, dtype=jnp.int32)
    columns = jnp.concatenate(
        [jnp.arange(node_count, dtype=jnp.int32), node_count + packed // 16 * 4 + packed % 4]
    )
    source_hot = (neighbour[:, :, None] == columns).astype(jnp.bfloat16)
    live = (neighbour >= 0).astype(jnp.float32)[:, :, None]
    send_nodes = jnp.tile(mesh_send[0][:, None, :], (1, 4, 1)).reshape(-1)
    send_hot = send_nodes[:, None] == jnp.arange(node_count, dtype=jnp.int32)
    mapped = run_sections(
        states,
        edges,
        nodes,
        gains,
        source_hot,
        live,
        send_hot.astype(jnp.bfloat16),
        decode_weight,
        decode_other,
        owners,
    )

    gathered = gather_nodes(mapped).reshape(owners, node_count // block_size, block_size, features)
    chosen = gathered[jnp.arange(owners), decode_block[:, 0]].reshape(owners * block_size, features)
    cells = decode_source.reshape(3, blocks, 2, part_rows)

    def outputs(half):
        indices = lax.dynamic_index_in_dim(cells, half, 2, keepdims=False).reshape(3, -1)
        ids = jnp.arange(owners * block_size, dtype=jnp.int32)[None, :]
        counts = sum((indices[e][:, None] == ids).astype(jnp.float32) for e in range(3))
        summed = jnp.dot(counts.astype(jnp.bfloat16), chosen, preferred_element_type=jnp.float32)
        hidden = jax.nn.silu(summed).astype(jnp.bfloat16)
        return jnp.dot(hidden, output_all, preferred_element_type=jnp.float32)

    leaving = outputs(1 - phase_index).astype(jnp.bfloat16)
    arriving = swap(leaving).astype(jnp.float32)
    kept = outputs(phase_index)
    skipped = jnp.einsum(
        "mgrd,do->mgro", grid_fields, skip_weight, preferred_element_type=jnp.float32
    )
    here = (jnp.arange(2) == phase_index)[:, None, None, None]
    shape = (1, blocks, part_rows, kept.shape[1])
    return jnp.where(here, kept.reshape(shape), arriving.reshape(shape)) + skipped


def on_device(grid_fields, *others):
    phases, batches = lax.axis_size("phase"), grid_fields.shape[0]
    owners = lax.axis_size("shard")
    if phases == batches == 2 and owners == DEPTH * ROWS * CORES and others[7].shape[2] == 4 and others[10].shape[2] == 1:
        return on_device_batches(grid_fields, *others)
    return on_device_sections(grid_fields, *others)


def solution(mesh):
    return jax.shard_map(
        on_device,
        mesh=mesh,
        in_specs=(
            P(None, "shard", "phase", None),
            P(),
            P("shard", None, None),
            P("shard", None),
            P("shard", None, None, None),
            P("phase", None, None),
            P("phase", None, None),
            P("phase", None),
            P("shard", None, None),
            P("shard", None),
            P(None, "phase"),
            P("shard", None, None),
            P(None, "shard"),
            P("phase", None),
            P(),
        ),
        out_specs=P(None, "shard", "phase", None),
        check_vma=False,
    )
```

```python
import math

import jax
import jax.numpy as jnp
from jax import lax
from jax.experimental import pallas as pl
from jax.experimental.pallas import tpu as pltpu
from jax.sharding import PartitionSpec as P


def from_behind(value, axis, by):
    length = lax.axis_size(axis)
    pairs = [(i, i + by) for i in range(length) if 0 <= i + by < length]
    return lax.ppermute(value, axis, pairs)


def broadcast(block, axis, source):
    block = jnp.where(lax.axis_index(axis) == source, block, jnp.zeros_like(block))
    return lax.psum(block, axis)


def layer_norm(values):
    average = jnp.mean(values, axis=-1, keepdims=True)
    centred = values - average
    variance = jnp.mean(centred * centred, axis=-1, keepdims=True)
    return centred * lax.rsqrt(variance + 1e-05)


def add_by_target(values, targets, node_count):
    row_count, columns = values.shape
    block_rows = math.gcd(row_count, 2048)
    value_blocks = values.reshape(row_count // block_rows, block_rows, columns)
    target_blocks = targets.reshape(row_count // block_rows, block_rows)
    node_ids = jnp.arange(node_count, dtype=jnp.int32)

    def accumulate(running, pieces):
        onehot = (pieces[1][None, :] == node_ids[:, None]).astype(jnp.bfloat16)
        return (running + jnp.dot(onehot, pieces[0], preferred_element_type=jnp.float32), None)

    running, unused = lax.scan(
        accumulate, jnp.zeros((node_count, columns), jnp.float32), (value_blocks, target_blocks)
    )
    return running


def encode_sums(messages, send_blocks, slot_live, targets, node_count):
    picked = messages[send_blocks]
    picked = jnp.where(slot_live[:, :, None, None, None], picked, jnp.zeros_like(picked))
    arrived = lax.all_to_all(picked, "shard", split_axis=0, concat_axis=0, tiled=True)
    peer_count, capacity, part_rows, batches, columns = arrived.shape
    node_ids = jnp.where(targets >= 0, targets, node_count).reshape(-1)
    summed = add_by_target(
        arrived.reshape(peer_count * capacity * part_rows, batches * columns), node_ids, node_count
    )
    return jnp.transpose(summed.reshape(node_count, batches, columns), (1, 0, 2))


def on_device_sections(
    grid_fields,
    encode_weight,
    encode_send,
    encode_count,
    encode_target,
    edge_weight,
    node_weight,
    node_gain,
    mesh_send,
    mesh_neighbour,
    decode_weight,
    decode_send,
    decode_source,
    output_weight,
    skip_weight,
):
    phases = lax.axis_size("phase")
    phase_index = lax.axis_index("phase")
    batches, blocks, part_rows, features = grid_fields.shape
    node_count = mesh_neighbour.shape[0]
    block_size = encode_target.shape[3]
    send_blocks = encode_send[0]
    capacity = send_blocks.shape[1]
    slot_live = jnp.arange(capacity, dtype=jnp.int32)[None, :] < encode_count[0][:, None]
    messages = jax.nn.silu(
        jnp.einsum("mgrd,dc->grmc", grid_fields, encode_weight, preferred_element_type=jnp.float32)
    ).astype(jnp.bfloat16)
    own_targets = lax.dynamic_slice_in_dim(encode_target[0], phase_index * part_rows, part_rows, 2)
    partial_sums = encode_sums(messages, send_blocks, slot_live, own_targets, node_count)
    encoded = lax.psum(partial_sums, "phase")
    initial = layer_norm(encoded).astype(jnp.bfloat16)
    my_edge = edge_weight[0]
    my_node = node_weight[0]
    my_gain = node_gain[0]
    send_nodes = mesh_send[0]
    edge_live = mesh_neighbour >= 0
    safe_index = jnp.where(edge_live, mesh_neighbour, 0)
    slot_count = mesh_neighbour.shape[1]

    def process(mesh_state):
        both_parts = jnp.dot(mesh_state, my_edge, preferred_element_type=jnp.float32)
        source_part = both_parts[:, :features].astype(jnp.bfloat16)
        dest_part = both_parts[:, features:]
        incoming = lax.all_to_all(
            source_part[send_nodes], "shard", split_axis=0, concat_axis=0, tiled=True
        )
        lookup_table = jnp.concatenate([source_part, incoming.reshape(-1, features)], axis=0)
        running = jnp.zeros((node_count, features), jnp.float32)
        for slot_index in range(slot_count):
            gathered = lookup_table[safe_index[:, slot_index]].astype(jnp.float32)
            running = running + jnp.where(
                edge_live[:, slot_index][:, None], jax.nn.silu(gathered + dest_part), 0.0
            )
        summary = running.astype(jnp.bfloat16)
        mixed = jnp.dot(mesh_state, my_node[:features], preferred_element_type=jnp.float32)
        mixed = mixed + jnp.dot(summary, my_node[features:], preferred_element_type=jnp.float32)
        return (mesh_state.astype(jnp.float32) + my_gain * layer_norm(jax.nn.silu(mixed))).astype(
            jnp.bfloat16
        )

    tick_count = batches + phases - 1

    def advance(carried, tick_index):
        current, finished = carried
        entering = lax.dynamic_index_in_dim(
            initial, jnp.minimum(tick_index, batches - 1), 0, keepdims=False
        )
        inputs = jnp.where(phase_index == 0, entering, current)
        result = process(inputs)
        leaving = tick_index - (phases - 1)
        updated = lax.dynamic_update_index_in_dim(finished, result, jnp.maximum(leaving, 0), 0)
        finished = jnp.where((phase_index == phases - 1) & (leaving >= 0), updated, finished)
        current = from_behind(result, "phase", 1)
        return ((current, finished), None)

    carried, unused = lax.scan(
        advance,
        (jnp.zeros_like(initial[0]), jnp.zeros_like(initial)),
        jnp.arange(tick_count, dtype=jnp.int32),
    )
    finished = carried[1]
    final_states = broadcast(finished, "phase", phases - 1)
    mapped = jnp.einsum(
        "mnd,dc->nmc", final_states, decode_weight, preferred_element_type=jnp.float32
    ).astype(jnp.bfloat16)
    columns = mapped.shape[2]
    node_blocks = mapped.reshape(node_count // block_size, block_size, batches, columns)
    outgoing = node_blocks[decode_send[0]]
    arrived = lax.all_to_all(outgoing, "shard", split_axis=0, concat_axis=0, tiled=True)
    arrived = arrived.reshape(-1, batches, columns)
    summed = arrived[decode_source[0]].astype(jnp.float32)
    summed = summed + arrived[decode_source[1]].astype(jnp.float32)
    summed = summed + arrived[decode_source[2]].astype(jnp.float32)
    hidden = jax.nn.silu(summed).astype(jnp.bfloat16)
    skipped = jnp.einsum(
        "mgrd,do->mgro", grid_fields, skip_weight, preferred_element_type=jnp.float32
    )
    output_terms = jnp.einsum(
        "rmc,co->mro", hidden, output_weight, preferred_element_type=jnp.float32
    )
    output_terms = output_terms.reshape(batches, blocks, block_size, output_terms.shape[2])
    shared = lax.psum_scatter(output_terms, "phase", scatter_dimension=2, tiled=True)
    return shared + skipped


def swap(value):
    return lax.ppermute(value, "phase", [(0, 1), (1, 0)])


MESH_ID = pl.DeviceIdType.MESH
PIECE = 64
DEPTH, ROWS, CORES = 4, 2, 2


def greet(peers):
    barrier = pltpu.get_barrier_semaphore()
    for peer in peers:
        pl.semaphore_signal(barrier, inc=1, device_id=peer, device_id_type=MESH_ID)
    pl.semaphore_wait(barrier, len(peers))


def send(source, target, sems, at, peer):
    copy = pltpu.make_async_remote_copy(
        src_ref=source,
        dst_ref=target,
        send_sem=sems.at[0, at],
        recv_sem=sems.at[1, at],
        device_id=peer,
        device_id_type=MESH_ID,
    )
    copy.start()
    return copy


def places():
    phase, me = lax.axis_index("phase"), lax.axis_index("shard")
    z, y, c = me // 4, (me // 2) % 2, me % 2

    def at(z, y, c):
        return (phase, z * 4 + y * 2 + c)

    across = at(z, y, 1 - c)
    beside = at(z, 1 - y, c)
    line = [at((z + k) % DEPTH, y, c) for k in range(1, DEPTH)]
    return phase, me, z, y, c, across, beside, line


def owner_kernel(
    part, edge, node, decode, gain, states, edges, nodes, decode_other, gains,
    core_in, y_out, y_in, z_out, z_in, total, core_sems, y_sems, z_sems, weight_sems,
):
    phase, me, z, y, c, across, beside, line = places()
    partner = (1 - phase, me)
    keeps = [
        pltpu.make_async_copy(edge, edges.at[phase], weight_sems.at[0, 4]),
        pltpu.make_async_copy(node, nodes.at[phase], weight_sems.at[1, 4]),
        pltpu.make_async_copy(gain, gains.at[phase], weight_sems.at[0, 7]),
    ]
    for keep in keeps:
        keep.start()
    greet([across, beside, partner] + line)
    step = 32
    tiles = part.shape[3] // step
    order = (2, 1, 3, 0)
    spots = [(z + k) % DEPTH for k in range(DEPTH)]
    core_copies = {}
    for k in order:
        core_copies[k] = send(
            part.at[spots[k], :, 1 - c], core_in.at[spots[k]], core_sems, k, across
        )
    weight_copies = [
        send(edge.at[c], edges.at[phase, c], weight_sems, 0, partner),
        send(node.at[c], nodes.at[phase, c], weight_sems, 1, partner),
        send(decode, decode_other, weight_sems, 5, partner),
        send(gain, gains.at[phase], weight_sems, 6, partner),
    ]

    def over_tiles(body):
        def run(t, carry):
            body(pl.ds(pl.multiple_of(t * step, step), step))
            return carry

        lax.fori_loop(0, tiles, run, 0)

    def pair(spot, row, at):
        return part[spot, row, c, at, :].astype(jnp.float32) + core_in[spot, row, at, :].astype(
            jnp.float32
        )

    y_copies = {}
    for k in order:
        core_copies[k].wait()
        spot = spots[k]

        def to_beside(at):
            y_out[k, at, :] = pair(spot, 1 - y, at).astype(jnp.bfloat16)

        over_tiles(to_beside)
        y_copies[k] = send(y_out.at[k], y_in.at[k], y_sems, k, beside)
    z_copies = []
    for k in order:
        y_copies[k].wait()
        spot = spots[k]

        def add_up(at):
            value = pair(spot, y, at) + y_in[k, at, :].astype(jnp.float32)
            if k == 0:
                total[at, :] = value
            else:
                z_out[k - 1, at, :] = value.astype(jnp.bfloat16)

        over_tiles(add_up)
        if k:
            z_copies.append(send(z_out.at[k - 1], z_in.at[k - 1], z_sems, k - 1, line[k - 1]))
    for copy in weight_copies:
        copy.wait()
    weight_copies = [
        send(edges.at[1 - phase, c], edges.at[1 - phase, c], weight_sems, 2, across),
        send(nodes.at[1 - phase, c], nodes.at[1 - phase, c], weight_sems, 3, across),
    ]
    for copy in z_copies:
        copy.wait()

    def finish(at):
        value = total[at, :]
        for k in range(DEPTH - 1):
            value = value + z_in[k, at, :].astype(jnp.float32)
        states[at, :] = layer_norm(value).astype(jnp.bfloat16)

    over_tiles(finish)
    for copy in weight_copies + keeps:
        copy.wait()


def states_and_weights(partial_sums, edge, node, decode, gain):
    owners, nodes, features = partial_sums.shape
    part = partial_sums.reshape(DEPTH, ROWS, CORES, nodes, features)
    edge_half = edge.reshape(2, edge.shape[0] // 2, edge.shape[1])
    node_half = node.reshape(2, node.shape[0] // 2, node.shape[1])
    kind = jnp.bfloat16
    states, edges, node_weights, decode_other, gains = pl.pallas_call(
        owner_kernel,
        out_shape=(
            jax.ShapeDtypeStruct((nodes, features), kind),
            jax.ShapeDtypeStruct((2,) + edge_half.shape, kind),
            jax.ShapeDtypeStruct((2,) + node_half.shape, kind),
            jax.ShapeDtypeStruct(decode.shape, kind),
            jax.ShapeDtypeStruct((2,) + gain.shape, gain.dtype),
        ),
        in_specs=[pl.BlockSpec(memory_space=pltpu.VMEM)] * 5,
        out_specs=[pl.BlockSpec(memory_space=pltpu.VMEM)] * 5,
        scratch_shapes=[
            pltpu.VMEM((DEPTH, ROWS, nodes, features), kind),
            pltpu.VMEM((DEPTH, nodes, features), kind),
            pltpu.VMEM((DEPTH, nodes, features), kind),
            pltpu.VMEM((DEPTH - 1, nodes, features), kind),
            pltpu.VMEM((DEPTH - 1, nodes, features), kind),
            pltpu.VMEM((nodes, features), jnp.float32),
            pltpu.SemaphoreType.DMA((2, DEPTH)),
            pltpu.SemaphoreType.DMA((2, DEPTH)),
            pltpu.SemaphoreType.DMA((2, DEPTH - 1)),
            pltpu.SemaphoreType.DMA((2, 8)),
        ],
        compiler_params=pltpu.CompilerParams(
            collective_id=0, has_side_effects=True, vmem_limit_bytes=40 * 2**20
        ),
        name="sum_to_owners",
    )(part, edge_half, node_half, decode, gain)
    edges, node_weights = edges.reshape((2,) + edge.shape), node_weights.reshape((2,) + node.shape)
    return states, edges, node_weights, decode_other, gains


def gather_kernel(mine, everyone, own_sem, z_sems, y_sems, core_sems):
    phase, me, z, y, c, across, beside, line = places()
    greet([across, beside] + line)
    pieces = mine.shape[0] // PIECE
    whole = everyone.at[z, y, c]
    spans = [pl.ds(p * PIECE, PIECE) for p in range(pieces)]
    keep = pltpu.make_async_copy(mine, whole, own_sem.at[0])
    z_copies, y_copies, core_copies = {}, {}, []
    for p, span in enumerate(spans):
        own, here = mine.at[span], everyone.at[z, y, c, span]
        for k in (2, 1, 3):
            z_copies[p, k] = send(own, here, z_sems, p * 4 + k, line[k - 1])
        y_copies[p, 0] = send(own, here, y_sems, p * 4, beside)
        core_copies.append(send(own, here, core_sems, p * 8, across))
    keep.start()
    for p, span in enumerate(spans):
        for k in (1, 3, 2):
            z_copies[p, k].wait()
            block = everyone.at[(z + DEPTH - k) % DEPTH, y, c, span]
            y_copies[p, k] = send(block, block, y_sems, p * 4 + k, beside)
            core_copies.append(send(block, block, core_sems, p * 8 + k, across))
    for p, span in enumerate(spans):
        for k in (0, 1, 3, 2):
            y_copies[p, k].wait()
            block = everyone.at[(z + DEPTH - k) % DEPTH, 1 - y, c, span]
            core_copies.append(send(block, block, core_sems, p * 8 + 4 + k, across))
    keep.wait()
    for copy in core_copies:
        copy.wait()


def gather_nodes(mapped):
    pieces = mapped.shape[0] // PIECE
    return pl.pallas_call(
        gather_kernel,
        out_shape=jax.ShapeDtypeStruct((DEPTH, ROWS, CORES) + mapped.shape, mapped.dtype),
        in_specs=[pl.BlockSpec(memory_space=pltpu.VMEM)],
        out_specs=pl.BlockSpec(memory_space=pltpu.VMEM),
        scratch_shapes=[
            pltpu.SemaphoreType.DMA((1,)),
            pltpu.SemaphoreType.DMA((2, 4 * pieces)),
            pltpu.SemaphoreType.DMA((2, 4 * pieces)),
            pltpu.SemaphoreType.DMA((2, 8 * pieces)),
        ],
        compiler_params=pltpu.CompilerParams(
            collective_id=1, has_side_effects=True, vmem_limit_bytes=24 * 2**20
        ),
        name="gather_nodes",
    )(mapped)


def sum_rows_kernel(send_blocks, rows, targets, sums):
    owner = pl.program_id(0)
    block_size = rows.shape[1]
    nodes = lax.broadcasted_iota(jnp.int32, (sums.shape[1], block_size), 0)
    total = jnp.zeros(sums.shape[1:], jnp.float32)
    for slot in range(targets.shape[2] // block_size):
        wanted = targets[0, :, slot * block_size : (slot + 1) * block_size]
        hot = (nodes == wanted).astype(jnp.float32).astype(jnp.bfloat16)
        block = rows[send_blocks[owner, slot]]
        total = total + jnp.dot(hot, block, preferred_element_type=jnp.float32)
    sums[0] = total.astype(jnp.bfloat16)


def sum_rows(rows, send_blocks, targets, node_count):
    owners, width = targets.shape
    features = rows.shape[2]
    return pl.pallas_call(
        sum_rows_kernel,
        out_shape=jax.ShapeDtypeStruct((owners, node_count, features), jnp.bfloat16),
        grid_spec=pltpu.PrefetchScalarGridSpec(
            num_scalar_prefetch=1,
            grid=(owners,),
            in_specs=[
                pl.BlockSpec(rows.shape, lambda o, blocks: (0, 0, 0)),
                pl.BlockSpec((1, 1, width), lambda o, blocks: (o, 0, 0)),
            ],
            out_specs=pl.BlockSpec((1, node_count, features), lambda o, blocks: (o, 0, 0)),
        ),
        compiler_params=pltpu.CompilerParams(vmem_limit_bytes=24 * 2**20),
        name="sum_rows",
    )(send_blocks, rows, targets[:, None, :])


def silu(values):
    half = 0.5 * values
    return half + half * jnp.tanh(half)


def sections_kernel(
    first, edges, nodes, gains, source_hot, live, send_hot, decode, decode_other, mapped,
    states, outgoing, incoming, table, dest, mixed, running, send_sems, recv_sems,
):
    phase, me = lax.axis_index("phase"), lax.axis_index("shard")
    owners, lanes = incoming.shape[1], incoming.shape[3]
    node_count, features = first.shape
    slots = source_hot.shape[0]
    peers = [lax.rem(me + k, owners) for k in range(1, owners)]
    greet([(phase, peer) for peer in peers])
    packed = owners * 16
    chunk_of_row = (lax.broadcasted_iota(jnp.int32, (packed, lanes), 0) // 4) % 4
    states[...] = first[...]

    def dot(left, right):
        return jnp.dot(left, right, preferred_element_type=jnp.float32)

    for layer in range(2):
        source = dot(states[...], edges[layer, :, :features]).astype(jnp.bfloat16)
        table[:node_count, :] = source
        chosen = dot(send_hot[...], source)
        payload = jnp.zeros((packed, lanes), jnp.float32)
        for j in range(4):
            payload = jnp.where(chunk_of_row == j, chosen[:, j * lanes : (j + 1) * lanes], payload)
        outgoing[layer] = payload.astype(jnp.bfloat16).reshape(owners, 16, lanes)
        copies = []
        for k, peer in enumerate(peers):
            copy = pltpu.make_async_remote_copy(
                src_ref=outgoing.at[layer, peer],
                dst_ref=incoming.at[layer, me],
                send_sem=send_sems.at[layer, k],
                recv_sem=recv_sems.at[layer, k],
                device_id=(phase, peer),
                device_id_type=MESH_ID,
            )
            copy.start()
            copies.append(copy)
        incoming[layer, me] = outgoing[layer, me]
        dest[...] = dot(states[...], edges[layer, :, features:])
        mixed[...] = dot(states[...], nodes[layer, :features, :])
        running[...] = jnp.zeros_like(running)
        for copy in copies:
            copy.wait()
        arrived = incoming[layer].reshape(packed, lanes).astype(jnp.float32)
        for j in range(4):
            table[node_count:, j * lanes : (j + 1) * lanes] = jnp.where(
                chunk_of_row == j, arrived, 0.0
            ).astype(jnp.bfloat16)

        def one_slot(slot, carry):
            gathered = dot(source_hot[slot], table[...])
            running[...] += silu(gathered + dest[...]) * live[slot]
            return carry

        lax.fori_loop(0, slots, one_slot, 0)
        value = mixed[...] + dot(running[...].astype(jnp.bfloat16), nodes[layer, features:, :])
        value = gains[layer] * layer_norm(silu(value))
        states[...] = (states[...].astype(jnp.float32) + value).astype(jnp.bfloat16)
    width = decode.shape[1]
    mapped[:, :width] = dot(states[...], decode[...]).astype(jnp.bfloat16)
    mapped[:, width:] = dot(states[...], decode_other[...]).astype(jnp.bfloat16)


def run_sections(
    states, edges, nodes, gains, source_hot, live, send_hot, decode, decode_other, owners
):
    node_count, features = states.shape
    lanes = features // 4
    kind = jnp.bfloat16
    return pl.pallas_call(
        sections_kernel,
        out_shape=jax.ShapeDtypeStruct((node_count, features), kind),
        in_specs=[pl.BlockSpec(memory_space=pltpu.VMEM)] * 9,
        out_specs=pl.BlockSpec(memory_space=pltpu.VMEM),
        scratch_shapes=[
            pltpu.VMEM((node_count, features), kind),
            pltpu.VMEM((2, owners, 16, lanes), kind),
            pltpu.VMEM((2, owners, 16, lanes), kind),
            pltpu.VMEM((node_count + owners * 16, features), kind),
            pltpu.VMEM((node_count, features), jnp.float32),
            pltpu.VMEM((node_count, features), jnp.float32),
            pltpu.VMEM((node_count, features), jnp.float32),
            pltpu.SemaphoreType.DMA((2, owners - 1)),
            pltpu.SemaphoreType.DMA((2, owners - 1)),
        ],
        compiler_params=pltpu.CompilerParams(
            collective_id=2, has_side_effects=True, vmem_limit_bytes=40 * 2**20
        ),
        name="run_sections",
    )(states, edges, nodes, gains, source_hot, live, send_hot, decode, decode_other)


def on_device_batches(
    grid_fields,
    encode_weight,
    encode_send,
    encode_count,
    encode_target,
    edge_weight,
    node_weight,
    node_gain,
    mesh_send,
    mesh_neighbour,
    decode_weight,
    decode_send,
    decode_source,
    output_weight,
    skip_weight,
):
    phase_index = lax.axis_index("phase")
    owners = lax.axis_size("shard")
    batches, blocks, part_rows, features = grid_fields.shape
    node_count, slot_count = mesh_neighbour.shape
    block_size = encode_target.shape[3]
    send_blocks = encode_send[0]
    capacity = send_blocks.shape[1]

    messages = jax.nn.silu(
        jnp.einsum("mgrd,dc->mgrc", grid_fields, encode_weight, preferred_element_type=jnp.float32)
    ).astype(jnp.bfloat16)
    own = lax.dynamic_index_in_dim(messages, phase_index, 0, keepdims=False)
    away = lax.dynamic_index_in_dim(messages, 1 - phase_index, 0, keepdims=False)
    came = swap(away)
    rows = jnp.concatenate([own, came], axis=1)

    tables = jnp.concatenate(
        [encode_target[0].reshape(owners, -1), decode_send[0].reshape(owners, -1)], axis=1
    )
    tables = lax.all_to_all(tables, "shard", split_axis=0, concat_axis=0, tiled=True)
    targets = tables[:, : capacity * block_size].reshape(owners, capacity, 2, part_rows)
    decode_block = tables[:, capacity * block_size :]
    targets = jnp.where(phase_index == 0, targets, targets[:, :, ::-1])
    targets = targets.reshape(owners, capacity * block_size)
    slot_live = jnp.arange(capacity, dtype=jnp.int32)[None, :] < encode_count[0][:, None]
    live = jnp.repeat(slot_live, block_size, axis=1)
    targets = jnp.where(live, targets, -1)
    partial_sums = sum_rows(rows, send_blocks, targets, node_count)

    states, edges, nodes, decode_other, gains = states_and_weights(
        partial_sums, edge_weight[0], node_weight[0], decode_weight, node_gain
    )
    states, output_weight = lax.optimization_barrier((states, output_weight))
    output_other, width = swap(output_weight), output_weight.shape[0]

    neighbour = mesh_neighbour.T
    packed = jnp.arange(owners * 16, dtype=jnp.int32)
    columns = jnp.concatenate(
        [jnp.arange(node_count, dtype=jnp.int32), node_count + packed // 16 * 4 + packed % 4]
    )
    source_hot = (neighbour[:, :, None] == columns).astype(jnp.bfloat16)
    live = (neighbour >= 0).astype(jnp.float32)[:, :, None]
    send_nodes = jnp.tile(mesh_send[0][:, None, :], (1, 4, 1)).reshape(-1)
    send_hot = send_nodes[:, None] == jnp.arange(node_count, dtype=jnp.int32)
    mapped = run_sections(
        states,
        edges,
        nodes,
        gains,
        source_hot,
        live,
        send_hot.astype(jnp.bfloat16),
        decode_weight,
        decode_other,
        owners,
    )

    gathered = gather_nodes(mapped).reshape(owners, node_count // block_size, block_size, features)
    chosen = gathered[jnp.arange(owners), decode_block[:, 0]].reshape(owners * block_size, features)
    cells = decode_source.reshape(3, blocks, 2, part_rows)

    def outputs(half):
        indices = lax.dynamic_index_in_dim(cells, half, 2, keepdims=False).reshape(3, -1)
        ids = jnp.arange(owners * block_size, dtype=jnp.int32)[None, :]
        counts = sum((indices[e][:, None] == ids).astype(jnp.float32) for e in range(3))
        summed = jnp.dot(counts.astype(jnp.bfloat16), chosen, preferred_element_type=jnp.float32)
        hidden = jax.nn.silu(summed).astype(jnp.bfloat16)
        result = jnp.dot(hidden[:, :width], output_weight, preferred_element_type=jnp.float32)
        return result + jnp.dot(
            hidden[:, width:], output_other, preferred_element_type=jnp.float32
        )

    leaving = outputs(1 - phase_index).astype(jnp.bfloat16)
    arriving = swap(leaving).astype(jnp.float32)
    kept = outputs(phase_index)
    skipped = jnp.einsum(
        "mgrd,do->mgro", grid_fields, skip_weight, preferred_element_type=jnp.float32
    )
    here = (jnp.arange(2) == phase_index)[:, None, None, None]
    shape = (1, blocks, part_rows, kept.shape[1])
    return jnp.where(here, kept.reshape(shape), arriving.reshape(shape)) + skipped


def on_device(grid_fields, *others):
    phases, batches = lax.axis_size("phase"), grid_fields.shape[0]
    owners = lax.axis_size("shard")
    if phases == batches == 2 and owners == DEPTH * ROWS * CORES and others[7].shape[2] == 4 and others[10].shape[2] == 1:
        return on_device_batches(grid_fields, *others)
    return on_device_sections(grid_fields, *others)


def solution(mesh):
    return jax.shard_map(
        on_device,
        mesh=mesh,
        in_specs=(
            P(None, "shard", "phase", None),
            P(),
            P("shard", None, None),
            P("shard", None),
            P("shard", None, None, None),
            P("phase", None, None),
            P("phase", None, None),
            P("phase", None),
            P("shard", None, None),
            P("shard", None),
            P(None, "phase"),
            P("shard", None, None),
            P(None, "shard"),
            P("phase", None),
            P(),
        ),
        out_specs=P(None, "shard", "phase", None),
        check_vma=False,
    )
```
